512 devices in a mesh: row: 32 (over z, x_hi, core), col: 16 (over x_lo, y).
Axes of the slice: x: 4 (x_hi: 2, x_lo: 2; x = x_hi * 2 + x_lo), y: 8, z: 8, core: 2. Of those that a mesh axis runs over, the one named last changes fastest.
Arguments:
- trunk_in: bfloat16 [1536, 32768], P('col', 'row'), may hold values from -24 to 24
- conv_weight: bfloat16 [5, 1536, 1536], P(None, 'col'), may hold values from -0.0625 to 0.0625
- conv_bias: float32 [1536], P('col'), may hold values from -3 to 3
- norm_gain: float32 [1536], replicated, may hold values from 0.1 to 1.9
- pair_proj: bfloat16 [64, 1536], replicated, may hold values from -0.15625 to 0.15625
- pair_in: bfloat16 [2048, 512, 128], P('row', 'col'), may hold values from -6 to 6
- opm_weight: bfloat16 [1024, 128], replicated, may hold values from -0.1875 to 0.1875
- pair_bias: float32 [128], replicated, may hold values from -3 to 3
Outputs:
- trunk_out: bfloat16 [1536, 32768], P('col', 'row')
- pair_out: bfloat16 [2048, 512, 128], P('row', 'col')
The draws below stay inside these ranges and needn't reach their ends.
All inputs are finite; a program needn't handle non-finite values.
Results may differ from the reference program's by a relative error of at most 0.012.
Values may be sent and summed in bfloat16 or wider, within the bound.
A program may use at most 64 MiB of HBM per device.

```python
import math
import jax
import jax.numpy as jnp
from jax import lax

TRUNK_CHANNELS = 1536
KW = 5
DILATION_STEP = 8
POOL = 16
OPM = 32
PAIR = 128
TOTAL_TOKENS = 32768
PAIR_LEN = 512
PAIR_ROWS = 2048
POOL_DEV = 64
N_ROW = 32


def draw_trunk_in(key, part):
    first, second, third = jax.random.split(key, 3)
    base = jax.random.truncated_normal(first, -4.0, 4.0, (TRUNK_CHANNELS, TOTAL_TOKENS), jnp.float32)
    row_scale = jnp.exp(jax.random.uniform(second, (1, TOTAL_TOKENS), jnp.float32, math.log(0.3), math.log(3.0)))
    col_scale = jnp.exp(jax.random.uniform(third, (TRUNK_CHANNELS, 1), jnp.float32, math.log(0.5), math.log(2.0)))
    return (base * row_scale * col_scale).astype(jnp.bfloat16)


def steps_of(rng, dims, cuts, low, largest):
    def one(dim, parts):
        draws = jax.random.uniform(jax.random.fold_in(jax.random.fold_in(rng, 6), dim), (parts,), jnp.float32, low / len(cuts), largest / len(cuts))
        return jnp.repeat(jnp.exp(draws), dims[dim] // parts).reshape((-1,) + (1,) * (len(dims) - dim - 1))

    gain = one(*cuts[0])
    for cut in cuts[1:]:
        gain = gain * one(*cut)
    return gain


def centred(own_key, shape, deviation, most, cuts=(), dtype=jnp.bfloat16):
    drawn = jax.random.normal(own_key, shape, jnp.float32) * deviation
    if len(cuts) > 0:
        drawn = steps_of(own_key, shape, cuts, -0.22, 0.18) * drawn
    return jnp.clip(drawn, min=-most, max=most).astype(dtype)


def setup_inputs(seed: int = 0) -> dict:
    splits = jax.random.split(jax.random.key(seed), 9)
    trunk_in = draw_trunk_in(jax.random.fold_in(splits[8], 71), 0)
    conv_weight = centred(splits[1], (KW, TRUNK_CHANNELS, TRUNK_CHANNELS), (KW * TRUNK_CHANNELS) ** -0.5, 0.0625, ((1, 16),))
    conv_bias = centred(splits[2], (TRUNK_CHANNELS,), 0.5, 3.0, ((0, 16),), jnp.float32)
    norm_gain = jnp.clip(1.0 + 0.18 * jax.random.normal(splits[3], (TRUNK_CHANNELS,), jnp.float32), 0.1, 1.9)
    pair_proj = centred(splits[4], (2 * OPM, TRUNK_CHANNELS), TRUNK_CHANNELS ** -0.5, 0.15625)
    pair_in = centred(splits[5], (PAIR_ROWS, PAIR_LEN, PAIR), 1.0, 6.0, ((0, 32), (1, 16)))
    opm_weight = centred(splits[6], (OPM * OPM, PAIR), (OPM * OPM) ** -0.5, 0.1875)
    pair_bias = centred(splits[7], (PAIR,), 0.5, 3.0, (), jnp.float32)
    return {"trunk_in": trunk_in, "conv_weight": conv_weight, "conv_bias": conv_bias, "norm_gain": norm_gain, "pair_proj": pair_proj, "pair_in": pair_in, "opm_weight": opm_weight, "pair_bias": pair_bias}


EPSILON = 1e-05

def reference(trunk_in, conv_weight, conv_bias, norm_gain, pair_proj, pair_in, opm_weight, pair_bias):
    source = trunk_in.astype(jnp.float32)
    scale = lax.rsqrt(lax.optimization_barrier(jnp.mean(source * source, axis=0, keepdims=True)) + EPSILON)
    gelu_output = jax.nn.gelu(source * norm_gain[:, None] * scale).astype(jnp.bfloat16)
    padded_trunk = jnp.pad(gelu_output, ((0, 0), (2 * DILATION_STEP, 2 * DILATION_STEP)))
    conv_sum = jnp.zeros((TRUNK_CHANNELS, TOTAL_TOKENS), jnp.float32)
    for tap_offset in range(KW):
        shifted_rows = padded_trunk[:, tap_offset * DILATION_STEP:tap_offset * DILATION_STEP + TOTAL_TOKENS]
        conv_sum = conv_sum + jnp.dot(conv_weight[tap_offset], shifted_rows, preferred_element_type=jnp.float32)
    trunk_out = (source + conv_sum + conv_bias[:, None]).astype(jnp.bfloat16)
    pooled = trunk_out.astype(jnp.float32).reshape(TRUNK_CHANNELS, TOTAL_TOKENS // POOL, POOL).mean(axis=2).astype(jnp.bfloat16)
    pooled_f = pooled.astype(jnp.float32)
    projected = lax.dot_general(pooled, pair_proj, (((0,), (1,)), ((), ())), preferred_element_type=jnp.float32)
    sides = (projected * lax.rsqrt(lax.optimization_barrier(jnp.sum(pooled_f * pooled_f, axis=0)) / TRUNK_CHANNELS + EPSILON)[:, None]).astype(jnp.bfloat16)
    row_side = sides[:, :OPM]
    col_side = sides[:, OPM:]

    def one_block(block_index):
        row_start = (block_index * POOL_DEV).astype(jnp.int32)
        row_block = lax.dynamic_slice_in_dim(row_side, row_start, POOL_DEV, 0)
        window_start = (row_start // PAIR_LEN * PAIR_LEN).astype(jnp.int32)
        window_cols = lax.dynamic_slice_in_dim(col_side, window_start, PAIR_LEN, 0)
        base_tile = lax.dynamic_slice_in_dim(pair_in, row_start, POOL_DEV, 0)
        outer = (row_block.astype(jnp.float32)[:, None, :, None] * window_cols.astype(jnp.float32)[None, :, None, :]).astype(jnp.bfloat16)
        outer = outer.reshape(POOL_DEV * PAIR_LEN, OPM * OPM)
        update = jnp.dot(outer, opm_weight, preferred_element_type=jnp.float32).reshape(POOL_DEV, PAIR_LEN, PAIR)
        return (base_tile.astype(jnp.float32) + update + pair_bias).astype(jnp.bfloat16)
    blocks = lax.map(one_block, jnp.arange(N_ROW).astype(jnp.int32))
    pair_out = blocks.reshape(PAIR_ROWS, PAIR_LEN, PAIR)
    return (trunk_out, pair_out)
```

```python
import functools
import jax
import jax.numpy as jnp
from jax import lax
from jax.experimental import pallas as pl
from jax.experimental.pallas import tpu as pltpu
from jax.sharding import PartitionSpec as P

MESH = pl.DeviceIdType.MESH
F32 = jnp.float32
BF16 = jnp.bfloat16

CH = 1536
OWN = 96
SEG = 512
EXT = 640
NY = 8
NROW = 32
TAPS = 5
STEP = 8
EPSILON = 1e-05


def gelu(v):
    u = 0.7978845608028654 * (v + 0.044715 * (v * v * v))
    return (0.5 * v) * (1.0 + jnp.tanh(u))


def kernel(
    x_hbm, w_hbm, cb_ref, g_ref, pp_ref, pair_hbm, opm_ref, pb_ref,
    tout_hbm, pout_hbm,
    xv, wbuf, raw_a, raw_b, swap, edge, stat, cbuf, act, gain, sc, taps, acc, bcol,
    tv, pool, zpool, part, side, cside, e1, e2, rexp, cexp, pin, pov,
    local_sem, pout_sem,
    swap_sem, cb_sem, edge_sem, ring_sem, stat_sem, w_sem, sib_sem, tout_sem, part_sem, side_sem,
):
    r = lax.axis_index("row")
    c = lax.axis_index("col")
    x = c // NY
    y = c % NY
    core = r % 2
    up = (r + 1) % NROW
    down = (r + NROW - 1) % NROW
    partner = (r, (1 - x) * NY + y)
    across = (r + 2 - 4 * ((r // 2) % 2), (1 - x) * NY + y)
    sibling = (r + 1 - 2 * core, c)
    ypeer = [(r, x * NY + (y + j) % NY) for j in range(NY)]
    dest = ((r // 8) * 8 + y, 2 * (r % 8) + x)
    source = ((r // 8) * 8 + c // 2, (c % 2) * NY + r % 8)
    to_self = jnp.logical_and(dest[0] == r, dest[1] == c)
    my_edge = r + 2 * x * 1 - 1
    my_edge = (my_edge + NROW) % NROW

    def send(src, dst, sems, dev):
        return pltpu.make_async_remote_copy(
            src_ref=src, dst_ref=dst, send_sem=sems.at[0], recv_sem=sems.at[1],
            device_id=dev, device_id_type=MESH,
        )

    half = pl.ds(pl.multiple_of(SEG * x, 128), SEG)
    load_x = pltpu.make_async_copy(x_hbm, xv, local_sem.at[0])
    load_a = pltpu.make_async_copy(x_hbm.at[:, half], raw_a.at[y], local_sem.at[1])
    load_w = pltpu.make_async_copy(
        w_hbm, wbuf.at[:, pl.ds(pl.multiple_of(OWN * x, 32), OWN), :], local_sem.at[2]
    )
    load_p = pltpu.make_async_copy(pair_hbm, pin, local_sem.at[3])
    load_x.start()
    load_a.start()

    barrier = pltpu.get_barrier_semaphore()
    greet = [partner, across, sibling] + ypeer[1:] + [(my_edge, y), (my_edge, NY + y)]
    for dev in greet:
        pl.semaphore_signal(barrier, inc=1, device_id=dev, device_id_type=MESH)

    @pl.when(jnp.logical_not(to_self))
    def _():
        pl.semaphore_signal(barrier, inc=1, device_id=source, device_id_type=MESH)

    cbuf[pl.ds(x, 1)] = jnp.broadcast_to(cb_ref[...], (1, 8, 128))
    load_x.wait()
    load_a.wait()
    pl.semaphore_wait(barrier, len(greet) + jnp.where(to_self, 0, 1))

    sent = []

    def go(copy):
        copy.start()
        sent.append(copy)
        return copy

    def ring(direction, kind, dist):
        buf = (raw_a, raw_b)[kind]
        if direction == 0:
            owner, dev = (y + NY - (dist - 1)) % NY, ypeer[1]
        else:
            owner, dev = (y + dist - 1) % NY, ypeer[NY - 1]
        return send(buf.at[owner], buf.at[owner], ring_sem.at[direction, kind, dist - 1], dev)

    def arrived(direction, kind, dist):
        buf = (raw_a, raw_b)[kind]
        owner = (y + NY - dist) % NY if direction == 0 else (y + dist) % NY
        send(buf.at[owner], buf.at[owner], ring_sem.at[direction, kind, dist - 1], ypeer[1]).wait_recv()

    other = 1 - x
    copy_swap = go(send(
        xv.at[:, pl.ds(pl.multiple_of(384 * other, 128), EXT)], swap, swap_sem, partner
    ))
    edge_up = send(xv.at[:, 896:1024], edge.at[x], edge_sem.at[x], (up, y))
    edge_down = send(xv.at[:, 0:128], edge.at[x], edge_sem.at[2 + x], (down, NY + y))
    edge_up.start()
    edge_down.start()
    go(ring(0, 0, 1))
    go(ring(1, 0, 1))
    copy_cb = go(send(cbuf.at[x], cbuf.at[x], cb_sem, partner))
    quarters = [pl.ds(pl.multiple_of(768 * core + 384 * q, 128), 384) for q in range(2)]
    mine = pl.ds(pl.multiple_of(OWN * x, 32), OWN)
    theirs = pl.ds(pl.multiple_of(OWN * other, 32), OWN)
    for q, dev in enumerate((partner, across)):
        go(send(w_hbm.at[:, :, quarters[q]], wbuf.at[:, mine, quarters[q]], w_sem.at[q], dev))
    load_w.start()
    load_p.start()

    copy_swap.wait_recv()
    for k in range(2):

        @pl.when(x == 0)
        def _():
            send(xv.at[:, 896:1024], edge.at[k], edge_sem.at[k], (up, y)).wait_recv()

        @pl.when(x == 1)
        def _():
            send(xv.at[:, 0:128], edge.at[k], edge_sem.at[2 + k], (up, y)).wait_recv()

    raw_b[y, 0:OWN, :] = swap[:, pl.ds(pl.multiple_of(128 * x, 128), SEG)]
    own_f = xv[:, half].astype(F32)
    their_f = raw_b[y, 0:OWN, :].astype(F32)
    sums = jnp.sum(own_f * own_f + their_f * their_f, axis=0, keepdims=True)
    at_end = jnp.logical_or(
        jnp.logical_and(x == 0, r == 0), jnp.logical_and(x == 1, r == NROW - 1)
    )
    lane = lax.broadcasted_iota(jnp.int32, (OWN, 128), 1)
    pick_inner = (lane < 64) == (x == 0)
    inner_a = xv[:, pl.ds(pl.multiple_of(SEG - 128 * x, 128), 128)].astype(F32)
    inner_b = swap[:, pl.ds(pl.multiple_of(SEG * other, 128), 128)].astype(F32)
    keep = jnp.where(at_end, 0.0, 1.0)
    outer_a = edge[x].astype(F32) * keep
    outer_b = edge[other].astype(F32) * keep
    halo_a = jnp.where(pick_inner, inner_a, outer_a)
    halo_b = jnp.where(pick_inner, inner_b, outer_b)
    halo_sums = jnp.sum(halo_a * halo_a + halo_b * halo_b, axis=0, keepdims=True)
    stat[y] = jnp.concatenate(
        [sums[:, 128 * t : 128 * t + 128] for t in range(4)]
        + [halo_sums, jnp.zeros((3, 128), F32)],
        axis=0,
    )
    for j in range(1, NY):
        go(send(stat.at[y], stat.at[y], stat_sem.at[j], ypeer[j]))
    lane48 = lax.broadcasted_iota(jnp.int32, (48, 128), 1)
    packed = halo_a[0:48]
    for q, piece in ((1, halo_a[48:96]), (2, halo_b[0:48]), (3, halo_b[48:96])):
        moved = pltpu.roll(piece, 32 * q, 1)
        inside = jnp.logical_and(lane48 >= 32 * q - 16, lane48 < 32 * q + 16)
        packed = jnp.where(inside, moved, packed)
    packed = packed.astype(BF16)
    for t in range(3):
        raw_b[y, OWN : OWN + 16, 128 * t : 128 * t + 128] = packed[16 * t : 16 * t + 16]
    raw_b[y, OWN : OWN + 16, 384:512] = jnp.zeros((16, 128), BF16)
    go(ring(0, 1, 1))
    go(ring(1, 1, 1))

    for i in range(12):
        gain[128 * i : 128 * i + 128, :] = jnp.transpose(
            jnp.broadcast_to(g_ref[i : i + 1, :], (128, 128))
        )
    arrived(0, 0, 1)
    go(ring(0, 0, 2))
    arrived(1, 0, 1)
    go(ring(1, 0, 2))
    token = lax.broadcasted_iota(jnp.int32, (SEG, 128), 0) // 16
    cell = lax.broadcasted_iota(jnp.int32, (SEG, 128), 1) % 32
    pool[...] = jnp.where(token == cell, 0.0625, 0.0).astype(BF16)
    zpool[...] = jnp.zeros(zpool.shape, BF16)
    entry = lax.broadcasted_iota(jnp.int32, (32, 1024), 0)
    column = lax.broadcasted_iota(jnp.int32, (32, 1024), 1)
    e1[...] = jnp.where(column // 32 == entry, 1.0, 0.0).astype(BF16)
    e2[...] = jnp.where(column % 32 == entry, 1.0, 0.0).astype(BF16)
    copy_cb.wait_recv()
    for k in range(2):
        bcol[OWN * k : OWN * k + OWN, :] = jnp.transpose(
            jnp.broadcast_to(cbuf[k, 0:1, :], (128, 128))
        )[0:OWN]

    total = stat[y]
    for j in range(1, NY):
        send(stat.at[y], stat.at[(y + NY - j) % NY], stat_sem.at[j], ypeer[j]).wait_recv()
        total = total + stat[(y + NY - j) % NY]
    sc[...] = lax.rsqrt(total * (1.0 / CH) + EPSILON)

    def first_row(kind, owner):
        return ((x if kind == 0 else other) * NY + owner) * OWN

    def activate(kind, owner):
        buf = (raw_a, raw_b)[kind]
        base = first_row(kind, owner)

        def body(b, carry):
            rows = pl.ds(pl.multiple_of(b * 32, 32), 32)
            target = pl.ds(pl.multiple_of(base + b * 32, 32), 32)
            g = gain[target, :]
            for t in range(4):
                cols = slice(128 * t, 128 * t + 128)
                v = buf[owner, rows, cols].astype(F32) * g * sc[t : t + 1, :]
                act[target, cols] = gelu(v).astype(BF16)
            return carry

        lax.fori_loop(0, 3, body, 0)

    def activate_halo(owner):
        block = jnp.concatenate(
            [
                raw_b[owner, OWN : OWN + 16, 128 * t : 128 * t + 128].astype(F32)
                for t in range(3)
            ],
            axis=0,
        )
        for q in range(4):
            piece = block if q == 0 else pltpu.roll(block, 128 - 32 * q, 1)
            base = first_row(q // 2, owner) + 48 * (q % 2)
            target = pl.ds(pl.multiple_of(base, 16), 48)
            v = piece * gain[target, :] * sc[4:5, :]
            act[target, SEG:EXT] = gelu(v).astype(BF16)

    def behind(d):
        return (y + NY - d) % NY

    def ahead(d):
        return (y + d) % NY

    arrived(0, 1, 1)
    go(ring(0, 1, 2))
    arrived(1, 1, 1)
    go(ring(1, 1, 2))
    activate(0, y)
    activate(1, y)
    activate_halo(y)
    activate(0, behind(1))
    activate(0, ahead(1))
    arrived(0, 0, 2)
    go(ring(0, 0, 3))
    arrived(1, 0, 2)
    go(ring(1, 0, 3))
    activate(1, behind(1))
    activate(1, ahead(1))
    activate_halo(behind(1))
    activate_halo(ahead(1))
    arrived(0, 1, 2)
    go(ring(0, 1, 3))
    arrived(1, 1, 2)
    go(ring(1, 1, 3))
    activate(0, behind(2))
    activate(0, ahead(2))
    arrived(0, 0, 3)
    go(ring(0, 0, 4))
    arrived(1, 0, 3)
    for q in range(2):
        send(
            w_hbm.at[:, :, quarters[q]], wbuf.at[:, theirs, quarters[q]], w_sem.at[q], partner
        ).wait_recv()
    k_half = pl.ds(pl.multiple_of(768 * core, 128), 768)
    k_rest = pl.ds(pl.multiple_of(768 * (1 - core), 128), 768)
    go(send(wbuf.at[:, theirs, k_half], wbuf.at[:, theirs, k_half], sib_sem, sibling))
    activate(1, behind(2))
    activate(1, ahead(2))
    activate_halo(behind(2))
    activate_halo(ahead(2))
    activate(0, behind(3))
    activate(0, ahead(3))
    arrived(0, 1, 3)
    arrived(1, 1, 3)
    go(ring(1, 1, 4))
    activate(1, behind(3))
    activate(1, ahead(3))
    activate_halo(behind(3))
    activate_halo(ahead(3))
    load_w.wait()
    send(wbuf.at[:, theirs, k_rest], wbuf.at[:, theirs, k_rest], sib_sem, sibling).wait_recv()

    def product(tap, group):
        out = None
        for k in range(2):
            span = pl.ds(pl.multiple_of(768 * k + 384 * group, 128), 384)
            term = jnp.dot(wbuf[tap, :, span], act[span, :], preferred_element_type=F32)
            out = term if out is None else out + term
        return out

    group = y // 4

    def early(tap, carry):
        taps[tap] = product(tap, group)
        return carry

    lax.fori_loop(0, TAPS, early, 0)

    arrived(0, 0, 4)
    activate(0, behind(4))
    arrived(1, 1, 4)
    activate(1, ahead(4))
    activate_halo(ahead(4))

    for tap in range(TAPS):
        full = taps[tap] + product(tap, 1 - group)
        delta = STEP * (tap - 2)
        if delta != 0:
            full = pltpu.roll(full, (-delta) % EXT, 1)
        full = full[:, 0:SEG]
        if tap == 0:
            acc[...] = full
        else:
            acc[...] += full

    for t in range(4):
        cols = slice(128 * t, 128 * t + 128)
        own_cols = pl.ds(pl.multiple_of(SEG * x + 128 * t, 128), 128)
        tv[mine, cols] = (
            xv[:, own_cols].astype(F32) + acc[mine, cols] + bcol[mine, :]
        ).astype(BF16)
        tv[theirs, cols] = (
            raw_b[y, 0:OWN, cols].astype(F32) + acc[theirs, cols] + bcol[theirs, :]
        ).astype(BF16)
    copy_t = go(send(tv.at[theirs, :], tout_hbm.at[:, half], tout_sem, partner))
    store_t = pltpu.make_async_copy(tv.at[mine, :], tout_hbm.at[:, half], local_sem.at[4])
    store_t.start()
    pooled = jnp.dot(tv[...], pool[...], preferred_element_type=F32).astype(BF16)
    zpool[pl.ds(pl.multiple_of(OWN * y, 32), OWN), :] = pooled[0:OWN]
    zpool[pl.ds(pl.multiple_of(768 + OWN * y, 32), OWN), :] = pooled[OWN:]
    pooled_f = pooled.astype(F32)
    squares = jnp.sum(pooled_f * pooled_f, axis=0, keepdims=True)
    proj = jnp.dot(pp_ref[...], zpool[...], preferred_element_type=F32)
    lane16 = lax.broadcasted_iota(jnp.int32, (16, 128), 1) // 32
    folded = proj[0:16]
    for q in range(1, 4):
        folded = jnp.where(lane16 == q, proj[16 * q : 16 * q + 16], folded)
    part[y] = jnp.concatenate([folded, jnp.broadcast_to(squares, (8, 128))], axis=0)
    for j in range(1, NY):
        go(send(part.at[y], part.at[y], part_sem.at[j], ypeer[j]))
    whole = part[y]
    load_p.wait()
    for j in range(1, NY):
        frm = (y + NY - j) % NY
        send(part.at[y], part.at[frm], part_sem.at[j], ypeer[j]).wait_recv()
        whole = whole + part[frm]
    norm = lax.rsqrt(whole[16:17] * (1.0 / CH) + EPSILON)
    sides = (whole[0:16] * norm).astype(BF16)
    side[x] = sides
    copy_side = go(send(side.at[x], side.at[x], side_sem.at[0], partner))
    copy_c = send(side.at[x], cside, side_sem.at[1], dest)

    @pl.when(jnp.logical_not(to_self))
    def _():
        copy_c.start()

    copy_side.wait_recv()
    s0 = side[0].astype(F32)
    s1 = side[1].astype(F32)
    low = lax.broadcasted_iota(jnp.int32, (16, 128), 1) < 32
    row_t = jnp.concatenate(
        [
            jnp.where(low, s0, pltpu.roll(s1, 32, 1)),
            jnp.where(low, pltpu.roll(s0, 96, 1), s1),
        ],
        axis=0,
    )
    row_side = jnp.transpose(row_t)[0:64].astype(BF16)
    rexp[...] = jnp.dot(row_side, e1[...], preferred_element_type=F32)

    @pl.when(jnp.logical_not(to_self))
    def _():
        copy_c.wait_recv()

    @pl.when(to_self)
    def _():
        cside[...] = side[x]

    cs = cside[...].astype(F32)
    col_t = jnp.concatenate([pltpu.roll(cs, 64, 1), pltpu.roll(cs, 32, 1)], axis=0)
    col_side = jnp.transpose(col_t)[0:32].astype(BF16)
    cexp[...] = jnp.dot(col_side, e2[...], preferred_element_type=F32)

    def block(b, carry):
        rows = pl.ds(pl.multiple_of(b * 8, 8), 8)
        outer = jnp.concatenate(
            [(rexp[pl.ds(b * 8 + i, 1), :] * cexp[...]).astype(BF16) for i in range(8)], axis=0
        )
        update = jnp.dot(outer, opm_ref[...], preferred_element_type=F32)
        update = update.reshape(8, 32, 128)
        pov[rows] = (pin[rows].astype(F32) + update + pb_ref[...].reshape(1, 1, 128)).astype(BF16)
        pltpu.make_async_copy(pov.at[rows], pout_hbm.at[rows], pout_sem.at[b]).start()
        return carry

    lax.fori_loop(0, 8, block, 0)

    for b in range(8):
        rows = pl.ds(8 * b, 8)
        pltpu.make_async_copy(pov.at[rows], pout_hbm.at[rows], pout_sem.at[b]).wait()
    store_t.wait()
    other_half = pl.ds(pl.multiple_of(SEG * other, 128), SEG)
    send(tv.at[theirs, :], tout_hbm.at[:, other_half], tout_sem, partner).wait_recv()
    for copy in sent:
        copy.wait_send()
    edge_up.wait_send()
    edge_down.wait_send()

    @pl.when(jnp.logical_not(to_self))
    def _():
        copy_c.wait_send()


def per_device(trunk_in, conv_weight, conv_bias, norm_gain, pair_proj, pair_in, opm_weight, pair_bias):
    any_spec = pl.BlockSpec(memory_space=pl.ANY)
    vmem = pl.BlockSpec(memory_space=pltpu.VMEM)
    dma = pltpu.SemaphoreType.DMA
    bias_row = jnp.pad(conv_bias, (0, 128 - OWN)).reshape(1, 128)
    return pl.pallas_call(
        kernel,
        name="trunk_pair",
        out_shape=(
            jax.ShapeDtypeStruct(trunk_in.shape, BF16),
            jax.ShapeDtypeStruct(pair_in.shape, BF16),
        ),
        in_specs=[any_spec, any_spec, vmem, vmem, vmem, any_spec, vmem, vmem],
        out_specs=(any_spec, any_spec),
        scratch_shapes=[
            pltpu.VMEM((OWN, 1024), BF16),
            pltpu.VMEM((TAPS, 2 * OWN, CH), BF16),
            pltpu.VMEM((NY, OWN, SEG), BF16),
            pltpu.VMEM((NY, OWN + 16, SEG), BF16),
            pltpu.VMEM((OWN, EXT), BF16),
            pltpu.VMEM((2, OWN, 128), BF16),
            pltpu.VMEM((NY, 8, 128), F32),
            pltpu.VMEM((2, 8, 128), F32),
            pltpu.VMEM((CH, EXT), BF16),
            pltpu.VMEM((CH, 128), F32),
            pltpu.VMEM((8, 128), F32),
            pltpu.VMEM((TAPS, 2 * OWN, EXT), F32),
            pltpu.VMEM((2 * OWN, SEG), F32),
            pltpu.VMEM((2 * OWN, 128), F32),
            pltpu.VMEM((2 * OWN, SEG), BF16),
            pltpu.VMEM((SEG, 128), BF16),
            pltpu.VMEM((CH, 128), BF16),
            pltpu.VMEM((NY, 24, 128), F32),
            pltpu.VMEM((2, 16, 128), BF16),
            pltpu.VMEM((16, 128), BF16),
            pltpu.VMEM((32, 1024), BF16),
            pltpu.VMEM((32, 1024), BF16),
            pltpu.VMEM((64, 1024), F32),
            pltpu.VMEM((32, 1024), F32),
            pltpu.VMEM((64, 32, 128), BF16),
            pltpu.VMEM((64, 32, 128), BF16),
            dma((5,)),
            dma((8,)),
            dma((2,)),
            dma((2,)),
            dma((4, 2)),
            dma((2, 2, 4, 2)),
            dma((NY, 2)),
            dma((2, 2)),
            dma((2,)),
            dma((2,)),
            dma((NY, 2)),
            dma((2, 2)),
        ],
        compiler_params=pltpu.CompilerParams(
            collective_id=0, has_side_effects=True, vmem_limit_bytes=48 * 1024 * 1024
        ),
        cost_estimate=pl.CostEstimate(
            flops=2_000_000_000, bytes_accessed=4_000_000, transcendentals=1_000_000
        ),
    )(
        trunk_in, conv_weight, bias_row, norm_gain.reshape(12, 128), pair_proj, pair_in,
        opm_weight, pair_bias.reshape(1, 128),
    )


def solution(mesh):
    return jax.shard_map(
        per_device,
        mesh=mesh,
        in_specs=(
            P("col", "row"), P(None, "col", None), P("col"), P(), P(), P("row", "col", None), P(), P(),
        ),
        out_specs=(P("col", "row"), P("row", "col", None)),
        check_vma=False,
    )
```

```python
import functools
import jax
import jax.numpy as jnp
from jax import lax
from jax.experimental import pallas as pl
from jax.experimental.pallas import tpu as pltpu
from jax.sharding import PartitionSpec as P

MESH = pl.DeviceIdType.MESH
F32 = jnp.float32
BF16 = jnp.bfloat16

CH = 1536
OWN = 96
SEG = 512
EXT = 640
NY = 8
NROW = 32
TAPS = 5
STEP = 8
EPSILON = 1e-05


def gelu(v):
    u = 0.7978845608028654 * (v + 0.044715 * (v * v * v))
    return (0.5 * v) * (1.0 + jnp.tanh(u))


def kernel(
    x_hbm, w_hbm, cb_hbm, g_hbm, pp_hbm, opm_hbm,
    tout_hbm, sides_hbm, wide_hbm,
    xv, wbuf, raw_a, raw_b, swap, edge, hal, cbuf, act, gain, sc, taps, acc, bcol,
    tv, pool, zpool, part, side, cb_ref, g_ref, pp_ref, opm_ref, opm_f, wide,
    local_sem,
    swap_sem, cb_sem, edge_sem, ring_sem, hal_sem, w_sem, sib_sem, tout_sem, part_sem, side_sem,
):
    r = lax.axis_index("row")
    c = lax.axis_index("col")
    x = c // NY
    y = c % NY
    core = r % 2
    up = (r + 1) % NROW
    down = (r + NROW - 1) % NROW
    partner = (r, (1 - x) * NY + y)
    across = (r + 2 - 4 * ((r // 2) % 2), (1 - x) * NY + y)
    sibling = (r + 1 - 2 * core, c)
    ypeer = [(r, x * NY + (y + j) % NY) for j in range(NY)]
    dest = ((r // 8) * 8 + y, 2 * (r % 8) + x)
    source = ((r // 8) * 8 + c // 2, (c % 2) * NY + r % 8)
    to_self = jnp.logical_and(dest[0] == r, dest[1] == c)
    my_edge = r + 2 * x * 1 - 1
    my_edge = (my_edge + NROW) % NROW

    def send(src, dst, sems, dev):
        return pltpu.make_async_remote_copy(
            src_ref=src, dst_ref=dst, send_sem=sems.at[0], recv_sem=sems.at[1],
            device_id=dev, device_id_type=MESH,
        )

    half = pl.ds(pl.multiple_of(SEG * x, 128), SEG)
    load_x = pltpu.make_async_copy(x_hbm, xv, local_sem.at[0])
    load_a = pltpu.make_async_copy(x_hbm.at[:, half], raw_a.at[y], local_sem.at[1])
    load_w = pltpu.make_async_copy(
        w_hbm, wbuf.at[:, pl.ds(pl.multiple_of(OWN * x, 32), OWN), :], local_sem.at[2]
    )
    tables = [
        pltpu.make_async_copy(src, dst, local_sem.at[5 + k])
        for k, (src, dst) in enumerate(
            ((cb_hbm, cb_ref), (g_hbm, g_ref), (pp_hbm, pp_ref), (opm_hbm, opm_ref))
        )
    ]
    load_x.start()
    load_a.start()
    for copy in tables[:2]:
        copy.start()

    barrier = pltpu.get_barrier_semaphore()
    diagonal = [(r, (1 - x) * NY + (y + j) % NY) for j in (1, NY - 1)]
    greet = [partner, across, sibling] + diagonal + ypeer[1:] + [(my_edge, y), (my_edge, NY + y)]
    for dev in greet:
        pl.semaphore_signal(barrier, inc=1, device_id=dev, device_id_type=MESH)

    @pl.when(jnp.logical_not(to_self))
    def _():
        pl.semaphore_signal(barrier, inc=1, device_id=source, device_id_type=MESH)

    cbuf[pl.ds(x, 1)] = jnp.zeros((1, 8, 128), F32)
    tables[0].wait()
    cbuf[pl.ds(x, 1), :, 0:OWN] = jnp.broadcast_to(cb_ref[...].reshape(1, 1, OWN), (1, 8, OWN))
    load_x.wait()
    load_a.wait()
    pl.semaphore_wait(barrier, len(greet) + jnp.where(to_self, 0, 1))

    sent = []

    def go(copy):
        copy.start()
        sent.append(copy)
        return copy

    def piece_of(kind, owner, piece):
        return (raw_a, raw_b)[kind].at[owner, 48 * piece : 48 * piece + 48]

    def ring(direction, kind, dist, piece):
        owner = (y + NY - (dist - 1)) % NY if direction == 0 else (y + dist - 1) % NY
        at = piece_of(kind, owner, piece)
        dev = ypeer[1] if direction == 0 else ypeer[NY - 1]
        src = at
        if kind == 1 and dist == 1:
            src = xv.at[48 * piece : 48 * piece + 48, other_half]
            dev = diagonal[direction]
        return send(src, at, ring_sem.at[direction, kind, dist - 1, piece], dev)

    def arrived(direction, kind, dist, piece):
        owner = (y + NY - dist) % NY if direction == 0 else (y + dist) % NY
        at = piece_of(kind, owner, piece)
        send(at, at, ring_sem.at[direction, kind, dist - 1, piece], ypeer[1]).wait_recv()

    def step(kind, dist, piece):
        if dist < 4 or kind == 0:
            arrived(0, kind, dist, piece)
            if dist < 3 or (dist == 3 and kind == 0):
                go(ring(0, kind, dist + 1, piece))
        if dist < 4 or kind == 1:
            arrived(1, kind, dist, piece)
            if dist < 3 or (dist == 3 and kind == 1):
                go(ring(1, kind, dist + 1, piece))

    other_half = pl.ds(pl.multiple_of(SEG * (1 - x), 128), SEG)
    other = 1 - x
    edge_up = send(xv.at[:, 896:1024], edge.at[x], edge_sem.at[x], (up, y))
    edge_down = send(xv.at[:, 0:128], edge.at[x], edge_sem.at[2 + x], (down, NY + y))
    edge_up.start()
    edge_down.start()
    for piece in range(2):
        for direction in range(2):
            go(ring(direction, 0, 1, piece))
    copy_swap = go(send(
        xv.at[:, pl.ds(pl.multiple_of(384 * other, 128), EXT)], swap, swap_sem, partner
    ))
    for piece in range(2):
        for direction in range(2):
            go(ring(direction, 1, 1, piece))
    copy_cb = go(send(cbuf.at[x], cbuf.at[x], cb_sem, partner))
    quarters = [pl.ds(pl.multiple_of(768 * core + 384 * q, 128), 384) for q in range(2)]
    mine = pl.ds(pl.multiple_of(OWN * x, 32), OWN)
    theirs = pl.ds(pl.multiple_of(OWN * other, 32), OWN)
    for q, dev in enumerate((partner, across)):
        go(send(w_hbm.at[:, :, quarters[q]], wbuf.at[:, mine, quarters[q]], w_sem.at[q], dev))
    load_w.start()
    for copy in tables[2:]:
        copy.start()

    tables[1].wait()
    for i in range(12):
        gain[128 * i : 128 * i + 128, :] = jnp.transpose(
            jnp.broadcast_to(g_ref[i : i + 1, :], (128, 128))
        )
    for piece in range(2):
        step(0, 1, piece)

    copy_swap.wait_recv()
    for k in range(2):

        @pl.when(x == 0)
        def _():
            send(xv.at[:, 896:1024], edge.at[k], edge_sem.at[k], (up, y)).wait_recv()

        @pl.when(x == 1)
        def _():
            send(xv.at[:, 0:128], edge.at[k], edge_sem.at[2 + k], (up, y)).wait_recv()

    raw_b[y, 0:OWN, :] = swap[:, pl.ds(pl.multiple_of(128 * x, 128), SEG)]
    own_f = xv[:, half].astype(F32)
    their_f = raw_b[y, 0:OWN, :].astype(F32)
    sums = jnp.sum(own_f * own_f + their_f * their_f, axis=0, keepdims=True)
    at_end = jnp.logical_or(
        jnp.logical_and(x == 0, r == 0), jnp.logical_and(x == 1, r == NROW - 1)
    )
    lane = lax.broadcasted_iota(jnp.int32, (OWN, 128), 1)
    pick_inner = (lane < 64) == (x == 0)
    inner_a = xv[:, pl.ds(pl.multiple_of(SEG - 128 * x, 128), 128)].astype(F32)
    inner_b = swap[:, pl.ds(pl.multiple_of(SEG * other, 128), 128)].astype(F32)
    keep = jnp.where(at_end, 0.0, 1.0)
    outer_a = edge[x].astype(F32) * keep
    outer_b = edge[other].astype(F32) * keep
    halo_a = jnp.where(pick_inner, inner_a, outer_a)
    halo_b = jnp.where(pick_inner, inner_b, outer_b)
    halo_sums = jnp.sum(halo_a * halo_a + halo_b * halo_b, axis=0, keepdims=True)
    lane48 = lax.broadcasted_iota(jnp.int32, (48, 128), 1)
    packed = halo_a[0:48]
    for q, piece in ((1, halo_a[48:96]), (2, halo_b[0:48]), (3, halo_b[48:96])):
        moved = pltpu.roll(piece, 32 * q, 1)
        inside = jnp.logical_and(lane48 >= 32 * q - 16, lane48 < 32 * q + 16)
        packed = jnp.where(inside, moved, packed)
    sums = jnp.concatenate(
        [sums[:, 128 * t : 128 * t + 128] for t in range(4)]
        + [halo_sums, jnp.zeros((3, 128), F32)],
        axis=0,
    )
    rest = sums - sums.astype(BF16).astype(F32)
    hal[y] = jnp.concatenate([packed, sums, rest], axis=0).astype(BF16)
    for j in range(1, NY):
        go(send(hal.at[y], hal.at[y], hal_sem.at[j], ypeer[j]))
    for piece in range(2):
        step(1, 1, piece)
    token = lax.broadcasted_iota(jnp.int32, (SEG, 128), 0) // 16
    cell = lax.broadcasted_iota(jnp.int32, (SEG, 128), 1) % 32
    pool[...] = jnp.where(token == cell, 0.0625, 0.0).astype(BF16)
    zpool[...] = jnp.zeros(zpool.shape, BF16)
    tables[3].wait()
    opm_f[...] = opm_ref[...].astype(F32)
    for v in range(32):
        wide[:, 128 * v : 128 * v + 128] = opm_f[pl.ds(v, 32, stride=32), :].astype(BF16)
    store_wide = pltpu.make_async_copy(wide, wide_hbm, local_sem.at[3])
    store_wide.start()
    copy_cb.wait_recv()
    for k in range(2):
        bcol[OWN * k : OWN * k + OWN, :] = jnp.transpose(
            jnp.broadcast_to(cbuf[k, 0:1, :], (128, 128))
        )[0:OWN]

    for piece in range(2):
        step(0, 2, piece)

    def sums_of(owner):
        both = hal[owner, 48:64, :].astype(F32)
        return both[0:8] + both[8:16]

    total = sums_of(y)
    for j in range(1, NY):
        frm = (y + NY - j) % NY
        send(hal.at[y], hal.at[frm], hal_sem.at[j], ypeer[j]).wait_recv()
        total = total + sums_of(frm)
    sc[...] = lax.rsqrt(total * (1.0 / CH) + EPSILON)

    def first_row(kind, owner):
        return ((x if kind == 0 else other) * NY + owner) * OWN

    def activate(kind, owner):
        buf = (raw_a, raw_b)[kind]
        base = first_row(kind, owner)

        def body(b, carry):
            rows = pl.ds(pl.multiple_of(b * 32, 32), 32)
            target = pl.ds(pl.multiple_of(base + b * 32, 32), 32)
            g = gain[target, :]
            for t in range(4):
                cols = slice(128 * t, 128 * t + 128)
                v = buf[owner, rows, cols].astype(F32) * g * sc[t : t + 1, :]
                act[target, cols] = gelu(v).astype(BF16)
            return carry

        lax.fori_loop(0, 3, body, 0)

    def activate_halo(owner):
        block = hal[owner, 0:48, :].astype(F32)
        for q in range(4):
            piece = block if q == 0 else pltpu.roll(block, 128 - 32 * q, 1)
            base = first_row(q // 2, owner) + 48 * (q % 2)
            target = pl.ds(pl.multiple_of(base, 16), 48)
            v = piece * gain[target, :] * sc[4:5, :]
            act[target, SEG:EXT] = gelu(v).astype(BF16)

    def behind(d):
        return (y + NY - d) % NY

    def ahead(d):
        return (y + d) % NY

    activate(0, y)
    activate(1, y)
    for piece in range(2):
        step(1, 2, piece)
    activate_halo(y)
    for owner in (behind(1), ahead(1)):
        activate(0, owner)
        activate(1, owner)
    for piece in range(2):
        step(0, 3, piece)
    for owner in (behind(1), ahead(1)):
        activate_halo(owner)
    for owner in (behind(2), ahead(2)):
        activate(0, owner)
    for piece in range(2):
        step(1, 3, piece)
    for q in range(2):
        send(
            w_hbm.at[:, :, quarters[q]], wbuf.at[:, theirs, quarters[q]], w_sem.at[q], partner
        ).wait_recv()
    k_half = pl.ds(pl.multiple_of(768 * core, 128), 768)
    k_rest = pl.ds(pl.multiple_of(768 * (1 - core), 128), 768)
    go(send(wbuf.at[:, theirs, k_half], wbuf.at[:, theirs, k_half], sib_sem, sibling))
    for owner in (behind(2), ahead(2)):
        activate(1, owner)
        activate_halo(owner)
    for owner in (behind(3), ahead(3)):
        activate(0, owner)
        activate(1, owner)
        activate_halo(owner)
    activate_halo(ahead(4))
    load_w.wait()
    send(wbuf.at[:, theirs, k_rest], wbuf.at[:, theirs, k_rest], sib_sem, sibling).wait_recv()

    def product(tap, group):
        out = None
        for k in range(2):
            span = pl.ds(pl.multiple_of(768 * k + 384 * group, 128), 384)
            term = jnp.dot(wbuf[tap, :, span], act[span, :], preferred_element_type=F32)
            out = term if out is None else out + term
        return out

    group = y // 4

    def early(tap, carry):
        taps[tap] = product(tap, group)
        return carry

    lax.fori_loop(0, TAPS, early, 0)

    for piece in range(2):
        step(0, 4, piece)
    activate(0, behind(4))
    for piece in range(2):
        step(1, 4, piece)
    activate(1, ahead(4))

    for tap in range(TAPS):
        full = taps[tap] + product(tap, 1 - group)
        delta = STEP * (tap - 2)
        if delta != 0:
            full = pltpu.roll(full, (-delta) % EXT, 1)
        full = full[:, 0:SEG]
        if tap == 0:
            acc[...] = full
        else:
            acc[...] += full

    tables[2].wait()

    for t in range(4):
        cols = slice(128 * t, 128 * t + 128)
        own_cols = pl.ds(pl.multiple_of(SEG * x + 128 * t, 128), 128)
        tv[mine, cols] = (
            xv[:, own_cols].astype(F32) + acc[mine, cols] + bcol[mine, :]
        ).astype(BF16)
        tv[theirs, cols] = (
            raw_b[y, 0:OWN, cols].astype(F32) + acc[theirs, cols] + bcol[theirs, :]
        ).astype(BF16)
    copy_t = go(send(tv.at[theirs, :], tout_hbm.at[:, half], tout_sem, partner))
    store_t = pltpu.make_async_copy(tv.at[mine, :], tout_hbm.at[:, half], local_sem.at[4])
    store_t.start()
    pooled = jnp.dot(tv[...], pool[...], preferred_element_type=F32).astype(BF16)
    zpool[pl.ds(pl.multiple_of(OWN * y, 32), OWN), :] = pooled[0:OWN]
    zpool[pl.ds(pl.multiple_of(768 + OWN * y, 32), OWN), :] = pooled[OWN:]
    pooled_f = pooled.astype(F32)
    squares = jnp.sum(pooled_f * pooled_f, axis=0, keepdims=True)
    proj = jnp.dot(pp_ref[...], zpool[...], preferred_element_type=F32)
    lane16 = lax.broadcasted_iota(jnp.int32, (16, 128), 1) // 32
    folded = proj[0:16]
    for q in range(1, 4):
        folded = jnp.where(lane16 == q, proj[16 * q : 16 * q + 16], folded)
    squares = jnp.broadcast_to(squares, (8, 128))
    rest = squares - squares.astype(BF16).astype(F32)
    part[y] = jnp.concatenate([folded, squares, rest], axis=0).astype(BF16)
    for j in range(1, NY):
        go(send(part.at[y], part.at[y], part_sem.at[j], ypeer[j]))
    whole = part[y].astype(F32)
    for j in range(1, NY):
        frm = (y + NY - j) % NY
        send(part.at[y], part.at[frm], part_sem.at[j], ypeer[j]).wait_recv()
        whole = whole + part[frm].astype(F32)
    norm = lax.rsqrt((whole[16:17] + whole[24:25]) * (1.0 / CH) + EPSILON)
    sides = (whole[0:16] * norm).astype(BF16)
    side[x] = sides
    copy_side = go(send(side.at[x], side.at[x], side_sem.at[0], partner))
    copy_c = send(side.at[x], side.at[2], side_sem.at[1], dest)

    @pl.when(jnp.logical_not(to_self))
    def _():
        copy_c.start()

    @pl.when(jnp.logical_not(to_self))
    def _():
        copy_c.wait_recv()

    @pl.when(to_self)
    def _():
        side[2] = side[x]

    copy_side.wait_recv()
    store_s = pltpu.make_async_copy(side, sides_hbm, local_sem.at[9])
    store_s.start()

    store_wide.wait()
    store_t.wait()
    send(tv.at[theirs, :], tout_hbm.at[:, other_half], tout_sem, partner).wait_recv()
    for copy in sent:
        copy.wait_send()
    edge_up.wait_send()
    edge_down.wait_send()

    @pl.when(jnp.logical_not(to_self))
    def _():
        copy_c.wait_send()

    store_s.wait()


def pair_kernel(
    trunk_hbm, sides_hbm, wide_hbm, pair_hbm, pb_hbm, tout_hbm, pout_hbm,
    side, wide, pin, pov, pb, mix, rows_t, sem, in_sem, out_sem,
):
    loads = [
        pltpu.make_async_copy(src, dst, sem.at[k])
        for k, (src, dst) in enumerate(((sides_hbm, side), (wide_hbm, wide), (pb_hbm, pb)))
    ]
    for copy in loads:
        copy.start()
    for b in range(4):
        span = pl.ds(16 * b, 16)
        pltpu.make_async_copy(pair_hbm.at[span], pin.at[span], in_sem.at[b]).start()
    copy_t = pltpu.make_async_copy(trunk_hbm, tout_hbm, sem.at[3])
    copy_t.start()
    v_of = lax.broadcasted_iota(jnp.int32, (32, 256), 0)
    column = lax.broadcasted_iota(jnp.int32, (32, 256), 1)
    spread = jnp.where(column // 8 == v_of, 1.0, 0.0).astype(BF16)
    loads[0].wait()
    s0 = side[0].astype(F32)
    s1 = side[1].astype(F32)
    cs = side[2].astype(F32)
    low = lax.broadcasted_iota(jnp.int32, (16, 128), 1) < 32
    row_t = jnp.concatenate(
        [
            jnp.where(low, s0, pltpu.roll(s1, 32, 1)),
            jnp.where(low, pltpu.roll(s0, 96, 1), s1),
        ],
        axis=0,
    )
    row_side = jnp.transpose(row_t)[0:64].astype(BF16)
    col_t = jnp.concatenate([pltpu.roll(cs, 64, 1), pltpu.roll(cs, 32, 1)], axis=0)
    col_side = jnp.transpose(col_t)[0:32].astype(BF16)
    repeated = jnp.dot(col_side, spread, preferred_element_type=F32)
    for i in range(8):
        mix[32 * i : 32 * i + 32, :] = jnp.where(column % 8 == i, repeated, 0.0).astype(BF16)
    loads[1].wait()
    rows_t[...] = jnp.dot(row_side, wide[...], preferred_element_type=F32)
    loads[2].wait()
    for g in range(8):
        if g % 2 == 0:
            span = pl.ds(8 * g, 16)
            pltpu.make_async_copy(pair_hbm.at[span], pin.at[span], in_sem.at[g // 2]).wait()
        stack = jnp.concatenate(
            [rows_t[8 * g : 8 * g + 8, 128 * v : 128 * v + 128] for v in range(32)], axis=0
        ).astype(BF16)
        update = jnp.dot(mix[...], stack, preferred_element_type=F32).reshape(8, 32, 128)
        span = slice(8 * g, 8 * g + 8)
        pov[span] = (pin[span].astype(F32) + update + pb[...].reshape(1, 1, 128)).astype(BF16)
        span = pl.ds(8 * g, 8)
        pltpu.make_async_copy(pov.at[span], pout_hbm.at[span], out_sem.at[g]).start()
    for g in range(8):
        span = pl.ds(8 * g, 8)
        pltpu.make_async_copy(pov.at[span], pout_hbm.at[span], out_sem.at[g]).wait()
    copy_t.wait()


VMEM_LIMIT = 60 * 1024 * 1024


def per_device(trunk_in, conv_weight, conv_bias, norm_gain, pair_proj, pair_in, opm_weight, pair_bias):
    hbm = pl.BlockSpec(memory_space=pltpu.HBM)
    dma = pltpu.SemaphoreType.DMA
    trunk, sides, wide = pl.pallas_call(
        kernel,
        name="trunk",
        out_shape=(
            jax.ShapeDtypeStruct(trunk_in.shape, BF16),
            jax.ShapeDtypeStruct((3, 16, 128), BF16),
            jax.ShapeDtypeStruct((32, 4096), BF16),
        ),
        in_specs=[hbm] * 6,
        out_specs=(hbm, hbm, hbm),
        scratch_shapes=[
            pltpu.VMEM((OWN, 1024), BF16),
            pltpu.VMEM((TAPS, 2 * OWN, CH), BF16),
            pltpu.VMEM((NY, OWN, SEG), BF16),
            pltpu.VMEM((NY, OWN, SEG), BF16),
            pltpu.VMEM((OWN, EXT), BF16),
            pltpu.VMEM((2, OWN, 128), BF16),
            pltpu.VMEM((NY, 64, 128), BF16),
            pltpu.VMEM((2, 8, 128), F32),
            pltpu.VMEM((CH, EXT), BF16),
            pltpu.VMEM((CH, 128), F32),
            pltpu.VMEM((8, 128), F32),
            pltpu.VMEM((TAPS, 2 * OWN, EXT), F32),
            pltpu.VMEM((2 * OWN, SEG), F32),
            pltpu.VMEM((2 * OWN, 128), F32),
            pltpu.VMEM((2 * OWN, SEG), BF16),
            pltpu.VMEM((SEG, 128), BF16),
            pltpu.VMEM((CH, 128), BF16),
            pltpu.VMEM((NY, 32, 128), BF16),
            pltpu.VMEM((3, 16, 128), BF16),
            pltpu.VMEM((1, OWN), F32),
            pltpu.VMEM((12, 128), F32),
            pltpu.VMEM((64, CH), BF16),
            pltpu.VMEM((1024, 128), BF16),
            pltpu.VMEM((1024, 128), F32),
            pltpu.VMEM((32, 4096), BF16),
            dma((10,)),
            dma((2,)),
            dma((2,)),
            dma((4, 2)),
            dma((2, 2, 4, 2, 2)),
            dma((NY, 2)),
            dma((2, 2)),
            dma((2,)),
            dma((2,)),
            dma((NY, 2)),
            dma((2, 2)),
        ],
        compiler_params=pltpu.CompilerParams(
            collective_id=0, has_side_effects=True, vmem_limit_bytes=VMEM_LIMIT
        ),
        cost_estimate=pl.CostEstimate(
            flops=1_600_000_000, bytes_accessed=3_000_000, transcendentals=1_000_000
        ),
    )(
        trunk_in, conv_weight, conv_bias.reshape(1, OWN), norm_gain.reshape(12, 128), pair_proj,
        opm_weight,
    )
    return pl.pallas_call(
        pair_kernel,
        name="pair",
        out_shape=(
            jax.ShapeDtypeStruct(trunk_in.shape, BF16),
            jax.ShapeDtypeStruct(pair_in.shape, BF16),
        ),
        in_specs=[hbm] * 5,
        out_specs=(hbm, hbm),
        scratch_shapes=[
            pltpu.VMEM((3, 16, 128), BF16),
            pltpu.VMEM((32, 4096), BF16),
            pltpu.VMEM((64, 32, 128), BF16),
            pltpu.VMEM((64, 32, 128), BF16),
            pltpu.VMEM((1, 128), F32),
            pltpu.VMEM((256, 256), BF16),
            pltpu.VMEM((64, 4096), F32),
            dma((4,)),
            dma((4,)),
            dma((8,)),
        ],
        compiler_params=pltpu.CompilerParams(vmem_limit_bytes=VMEM_LIMIT),
        cost_estimate=pl.CostEstimate(flops=200_000_000, bytes_accessed=2_000_000, transcendentals=0),
    )(trunk, sides, wide, pair_in, pair_bias.reshape(1, 128))


def solution(mesh):
    return jax.shard_map(
        per_device,
        mesh=mesh,
        in_specs=(
            P("col", "row"), P(None, "col", None), P("col"), P(), P(), P("row", "col", None), P(), P(),
        ),
        out_specs=(P("col", "row"), P("row", "col", None)),
        check_vma=False,
    )
```

```python
import functools
import jax
import jax.numpy as jnp
from jax import lax
from jax.experimental import pallas as pl
from jax.experimental.pallas import tpu as pltpu
from jax.sharding import PartitionSpec as P

MESH = pl.DeviceIdType.MESH
F32 = jnp.float32
BF16 = jnp.bfloat16

CH = 1536
OWN = 96
SEG = 512
EXT = 640
NY = 8
NROW = 32
TAPS = 5
STEP = 8
EPSILON = 1e-05


def gelu(v):
    u = v * (0.7978845608028654 + 0.035677408136300125 * (v * v))
    h = 0.5 * v
    return h + h * jnp.tanh(u)


def kernel(
    x_hbm, w_hbm, cb_hbm, g_hbm, pp_hbm, opm_hbm,
    tout_hbm, sides_out, wide_hbm,
    xv, wbuf, raw_a, raw_b, inner, edge, hal, stat, cbuf, act, gain, sc, taps, acc, bcol,
    tv, pool, own_pp, part, side, cb_ref, g_ref, pp_ref, opm_ref, opm_f, wide,
    local_sem,
    swap_sem, inner_sem, cb_sem, edge_sem, ring_sem, hal_sem, stat_sem, w_sem, sib_sem, tout_sem, part_sem, side_sem,
):
    r = lax.axis_index("row")
    c = lax.axis_index("col")
    x = c // NY
    y = c % NY
    core = r % 2
    up = (r + 1) % NROW
    down = (r + NROW - 1) % NROW
    partner = (r, (1 - x) * NY + y)
    across = (r + 2 - 4 * ((r // 2) % 2), (1 - x) * NY + y)
    sibling = (r + 1 - 2 * core, c)
    ypeer = [(r, x * NY + (y + j) % NY) for j in range(NY)]
    dest = ((r // 8) * 8 + y, 2 * (r % 8) + x)
    source = ((r // 8) * 8 + c // 2, (c % 2) * NY + r % 8)
    to_self = jnp.logical_and(dest[0] == r, dest[1] == c)
    my_edge = r + 2 * x * 1 - 1
    my_edge = (my_edge + NROW) % NROW

    def send(src, dst, sems, dev):
        return pltpu.make_async_remote_copy(
            src_ref=src, dst_ref=dst, send_sem=sems.at[0], recv_sem=sems.at[1],
            device_id=dev, device_id_type=MESH,
        )

    half = pl.ds(pl.multiple_of(SEG * x, 128), SEG)
    load_x = pltpu.make_async_copy(x_hbm, xv, local_sem.at[0])
    load_a = pltpu.make_async_copy(x_hbm.at[:, half], raw_a.at[y], local_sem.at[1])
    load_w = pltpu.make_async_copy(
        w_hbm, wbuf.at[:, pl.ds(pl.multiple_of(OWN * x, 32), OWN), :], local_sem.at[2]
    )
    tables = [
        pltpu.make_async_copy(src, dst, local_sem.at[5 + k])
        for k, (src, dst) in enumerate(
            ((cb_hbm, cb_ref), (g_hbm, g_ref), (pp_hbm, pp_ref), (opm_hbm, opm_ref))
        )
    ]
    load_x.start()
    load_a.start()
    for copy in tables[:2]:
        copy.start()

    barrier = pltpu.get_barrier_semaphore()
    greet = [partner, across, sibling] + ypeer[1:] + [(my_edge, y), (my_edge, NY + y)]
    for dev in greet:
        pl.semaphore_signal(barrier, inc=1, device_id=dev, device_id_type=MESH)

    @pl.when(jnp.logical_not(to_self))
    def _():
        pl.semaphore_signal(barrier, inc=1, device_id=source, device_id_type=MESH)

    cbuf[pl.ds(x, 1)] = jnp.zeros((1, 8, 128), F32)
    tables[0].wait()
    cbuf[pl.ds(x, 1), :, 0:OWN] = jnp.broadcast_to(cb_ref[...].reshape(1, 1, OWN), (1, 8, OWN))
    load_x.wait()
    load_a.wait()
    pl.semaphore_wait(barrier, len(greet) + jnp.where(to_self, 0, 1))

    sent = []

    def go(copy):
        copy.start()
        sent.append(copy)
        return copy

    def piece_of(kind, owner, piece):
        return (raw_a, raw_b)[kind].at[owner, 48 * piece : 48 * piece + 48]

    def ring(direction, kind, dist, piece):
        owner = (y + NY - (dist - 1)) % NY if direction == 0 else (y + dist - 1) % NY
        at = piece_of(kind, owner, piece)
        dev = ypeer[1] if direction == 0 else ypeer[NY - 1]
        return send(at, at, ring_sem.at[direction, kind, dist - 1, piece], dev)

    def arrived(direction, kind, dist, piece):
        owner = (y + NY - dist) % NY if direction == 0 else (y + dist) % NY
        at = piece_of(kind, owner, piece)
        send(at, at, ring_sem.at[direction, kind, dist - 1, piece], ypeer[1]).wait_recv()

    def step(kind, dist, piece):
        if dist < 4 or kind == 0:
            arrived(0, kind, dist, piece)
            if dist < 3 or (dist == 3 and kind == 0):
                go(ring(0, kind, dist + 1, piece))
        if dist < 4 or kind == 1:
            arrived(1, kind, dist, piece)
            if dist < 3 or (dist == 3 and kind == 1):
                go(ring(1, kind, dist + 1, piece))

    def halo_ring(direction, dist):
        owner = (y + NY - (dist - 1)) % NY if direction == 0 else (y + dist - 1) % NY
        dev = ypeer[1] if direction == 0 else ypeer[NY - 1]
        return send(hal.at[owner], hal.at[owner], hal_sem.at[direction, dist - 1], dev)

    def halo_step(dist):
        for direction in range(2 if dist < 4 else 1):
            owner = (y + NY - dist) % NY if direction == 0 else (y + dist) % NY
            at = hal.at[owner]
            send(at, at, hal_sem.at[direction, dist - 1], ypeer[1]).wait_recv()
            if dist < 3 or (dist == 3 and direction == 0):
                go(halo_ring(direction, dist + 1))

    other = 1 - x
    edge_up = send(xv.at[:, 896:1024], edge.at[x], edge_sem.at[x], (up, y))
    edge_down = send(xv.at[:, 0:128], edge.at[x], edge_sem.at[2 + x], (down, NY + y))
    edge_up.start()
    edge_down.start()
    for piece in range(2):
        for direction in range(2):
            go(ring(direction, 0, 1, piece))
    other_half = pl.ds(pl.multiple_of(SEG * other, 128), SEG)
    copy_swap = [
        go(send(
            xv.at[48 * p : 48 * p + 48, other_half], piece_of(1, y, p), swap_sem.at[p], partner
        ))
        for p in range(2)
    ]
    copy_inner = go(send(
        xv.at[:, pl.ds(pl.multiple_of(SEG - 128 * other, 128), 128)], inner, inner_sem, partner
    ))
    copy_cb = go(send(cbuf.at[x], cbuf.at[x], cb_sem, partner))
    quarters = [pl.ds(pl.multiple_of(768 * core + 384 * q, 128), 384) for q in range(2)]
    mine = pl.ds(pl.multiple_of(OWN * x, 32), OWN)
    theirs = pl.ds(pl.multiple_of(OWN * other, 32), OWN)
    for q, dev in enumerate((partner, across)):
        go(send(w_hbm.at[:, :, quarters[q]], wbuf.at[:, mine, quarters[q]], w_sem.at[q], dev))
    load_w.start()
    for copy in tables[2:]:
        copy.start()

    tables[1].wait()
    for i in range(12):
        gain[128 * i : 128 * i + 128, :] = jnp.transpose(
            jnp.broadcast_to(g_ref[i : i + 1, :], (128, 128))
        )
    for piece in range(2):
        step(0, 1, piece)
    for piece in range(2):
        copy_swap[piece].wait_recv()
        go(ring(0, 1, 1, piece))
        go(ring(1, 1, 1, piece))

    copy_inner.wait_recv()
    for k in range(2):

        @pl.when(x == 0)
        def _():
            send(xv.at[:, 896:1024], edge.at[k], edge_sem.at[k], (up, y)).wait_recv()

        @pl.when(x == 1)
        def _():
            send(xv.at[:, 0:128], edge.at[k], edge_sem.at[2 + k], (up, y)).wait_recv()

    own_f = xv[:, half].astype(F32)
    their_f = raw_b[y].astype(F32)
    sums = jnp.sum(own_f * own_f + their_f * their_f, axis=0, keepdims=True)
    at_end = jnp.logical_or(
        jnp.logical_and(x == 0, r == 0), jnp.logical_and(x == 1, r == NROW - 1)
    )
    lane = lax.broadcasted_iota(jnp.int32, (OWN, 128), 1)
    pick_inner = (lane < 64) == (x == 0)
    inner_a = xv[:, pl.ds(pl.multiple_of(SEG - 128 * x, 128), 128)].astype(F32)
    inner_b = inner[...].astype(F32)
    keep = jnp.where(at_end, 0.0, 1.0)
    outer_a = edge[x].astype(F32) * keep
    outer_b = edge[other].astype(F32) * keep
    halo_a = jnp.where(pick_inner, inner_a, outer_a)
    halo_b = jnp.where(pick_inner, inner_b, outer_b)
    halo_sums = jnp.sum(halo_a * halo_a + halo_b * halo_b, axis=0, keepdims=True)
    sums = jnp.concatenate(
        [sums[:, 128 * t : 128 * t + 128] for t in range(4)]
        + [halo_sums, jnp.zeros((3, 128), F32)],
        axis=0,
    )
    rest = sums - sums.astype(BF16).astype(F32)
    stat[y] = jnp.concatenate([sums, rest], axis=0).astype(BF16)
    for j in range(1, NY):
        go(send(stat.at[y], stat.at[y], stat_sem.at[j], ypeer[j]))
    lane48 = lax.broadcasted_iota(jnp.int32, (48, 128), 1)
    packed = halo_a[0:48]
    for q, piece in ((1, halo_a[48:96]), (2, halo_b[0:48]), (3, halo_b[48:96])):
        moved = pltpu.roll(piece, 32 * q, 1)
        inside = jnp.logical_and(lane48 >= 32 * q - 16, lane48 < 32 * q + 16)
        packed = jnp.where(inside, moved, packed)
    hal[y] = packed.astype(BF16)
    go(halo_ring(0, 1))
    go(halo_ring(1, 1))
    for piece in range(2):
        step(0, 2, piece)
    for piece in range(2):
        step(1, 1, piece)
    token = lax.broadcasted_iota(jnp.int32, (SEG, 128), 0) // 16
    cell = lax.broadcasted_iota(jnp.int32, (SEG, 128), 1) % 32
    pool[...] = jnp.where(token == cell, 0.0625, 0.0).astype(BF16)
    tables[2].wait()
    channel = lax.broadcasted_iota(jnp.int32, (CH, 2 * OWN), 0)
    place = lax.broadcasted_iota(jnp.int32, (CH, 2 * OWN), 1)
    wanted = place + OWN * y + jnp.where(place >= OWN, 768 - OWN, 0)
    choose = jnp.where(channel == wanted, 1.0, 0.0).astype(BF16)
    own_pp[...] = jnp.dot(pp_ref[...], choose, preferred_element_type=F32).astype(BF16)
    tables[3].wait()
    opm_f[...] = opm_ref[...].astype(F32)
    for v in range(32):
        wide[:, 128 * v : 128 * v + 128] = opm_f[pl.ds(v, 32, stride=32), :].astype(BF16)
    store_wide = pltpu.make_async_copy(wide, wide_hbm, local_sem.at[3])
    store_wide.start()
    copy_cb.wait_recv()
    for k in range(2):
        bcol[OWN * k : OWN * k + OWN, :] = jnp.transpose(
            jnp.broadcast_to(cbuf[k, 0:1, :], (128, 128))
        )[0:OWN]

    halo_step(1)

    def sums_of(owner):
        both = stat[owner].astype(F32)
        return both[0:8] + both[8:16]

    total = sums_of(y)
    for j in range(1, NY):
        frm = (y + NY - j) % NY
        send(stat.at[y], stat.at[frm], stat_sem.at[j], ypeer[j]).wait_recv()
        total = total + sums_of(frm)
    sc[...] = lax.rsqrt(total * (1.0 / CH) + EPSILON)

    def first_row(kind, owner):
        return ((x if kind == 0 else other) * NY + owner) * OWN

    def activate(kind, owner):
        buf = (raw_a, raw_b)[kind]
        base = first_row(kind, owner)

        for b in range(0, OWN, 16):
            target = pl.ds(pl.multiple_of(base + b, 16), 16)
            g = gain[target, :]
            for t in range(4):
                cols = slice(128 * t, 128 * t + 128)
                v = buf[owner, b : b + 16, cols].astype(F32) * g * sc[t : t + 1, :]
                act[target, cols] = gelu(v).astype(BF16)

    def activate_halo(owner):
        block = hal[owner].astype(F32)
        for q in range(4):
            piece = block if q == 0 else pltpu.roll(block, 128 - 32 * q, 1)
            base = first_row(q // 2, owner) + 48 * (q % 2)
            target = pl.ds(pl.multiple_of(base, 16), 48)
            v = piece * gain[target, :] * sc[4:5, :]
            act[target, SEG:EXT] = gelu(v).astype(BF16)

    def behind(d):
        return (y + NY - d) % NY

    def ahead(d):
        return (y + d) % NY

    for piece in range(2):
        step(0, 3, piece)
    activate(0, y)
    activate(1, y)
    for piece in range(2):
        step(1, 2, piece)
    halo_step(2)
    activate_halo(y)
    for owner in (behind(1), ahead(1)):
        activate(0, owner)
        activate(1, owner)
        activate_halo(owner)
    for owner in (behind(2), ahead(2)):
        activate(0, owner)
    for piece in range(2):
        step(1, 3, piece)
    halo_step(3)
    for q in range(2):
        send(
            w_hbm.at[:, :, quarters[q]], wbuf.at[:, theirs, quarters[q]], w_sem.at[q], partner
        ).wait_recv()
    k_half = pl.ds(pl.multiple_of(768 * core, 128), 768)
    k_rest = pl.ds(pl.multiple_of(768 * (1 - core), 128), 768)
    go(send(wbuf.at[:, theirs, k_half], wbuf.at[:, theirs, k_half], sib_sem, sibling))
    for owner in (behind(2), ahead(2)):
        activate(1, owner)
        activate_halo(owner)
    for owner in (behind(3), ahead(3)):
        activate(0, owner)
        activate(1, owner)
        activate_halo(owner)
    load_w.wait()
    send(wbuf.at[:, theirs, k_rest], wbuf.at[:, theirs, k_rest], sib_sem, sibling).wait_recv()

    def product(tap, group):
        out = None
        for k in range(2):
            span = pl.ds(pl.multiple_of(768 * k + 384 * group, 128), 384)
            term = jnp.dot(wbuf[tap, :, span], act[span, :], preferred_element_type=F32)
            out = term if out is None else out + term
        return out

    group = y // 4

    def early(tap, carry):
        taps[tap] = product(tap, group)
        return carry

    lax.fori_loop(0, TAPS, early, 0)

    for piece in range(2):
        step(0, 4, piece)
    activate(0, behind(4))
    halo_step(4)
    activate_halo(behind(4))
    for piece in range(2):
        step(1, 4, piece)
    activate(1, ahead(4))

    for tap in range(TAPS):
        full = taps[tap] + product(tap, 1 - group)
        delta = STEP * (tap - 2)
        if delta != 0:
            full = pltpu.roll(full, (-delta) % EXT, 1)
        full = full[:, 0:SEG]
        if tap == 0:
            acc[...] = full
        else:
            acc[...] += full

    for t in range(4):
        cols = slice(128 * t, 128 * t + 128)
        own_cols = pl.ds(pl.multiple_of(SEG * x + 128 * t, 128), 128)
        tv[mine, cols] = (
            xv[:, own_cols].astype(F32) + acc[mine, cols] + bcol[mine, :]
        ).astype(BF16)
        tv[theirs, cols] = (
            raw_b[y, :, cols].astype(F32) + acc[theirs, cols] + bcol[theirs, :]
        ).astype(BF16)
    pooled = jnp.dot(tv[...], pool[...], preferred_element_type=F32).astype(BF16)
    pooled_f = pooled.astype(F32)
    squares = jnp.sum(pooled_f * pooled_f, axis=0, keepdims=True)
    proj = jnp.dot(own_pp[...], pooled, preferred_element_type=F32)
    lane16 = lax.broadcasted_iota(jnp.int32, (16, 128), 1) // 32
    folded = proj[0:16]
    for q in range(1, 4):
        folded = jnp.where(lane16 == q, proj[16 * q : 16 * q + 16], folded)
    squares = jnp.broadcast_to(squares, (8, 128))
    rest = squares - squares.astype(BF16).astype(F32)
    part[y] = jnp.concatenate([folded, squares, rest], axis=0).astype(BF16)
    for j in range(1, NY):
        go(send(part.at[y], part.at[y], part_sem.at[j], ypeer[j]))
    copy_t = go(send(tv.at[theirs, :], tout_hbm.at[:, half], tout_sem, partner))
    store_t = pltpu.make_async_copy(tv.at[mine, :], tout_hbm.at[:, half], local_sem.at[4])
    store_t.start()
    whole = part[y].astype(F32)
    for j in range(1, NY):
        frm = (y + NY - j) % NY
        send(part.at[y], part.at[frm], part_sem.at[j], ypeer[j]).wait_recv()
        whole = whole + part[frm].astype(F32)
    norm = lax.rsqrt((whole[16:17] + whole[24:25]) * (1.0 / CH) + EPSILON)
    sides = (whole[0:16] * norm).astype(BF16)
    side[x] = sides
    copy_side = go(send(side.at[x], side.at[x], side_sem.at[0], partner))
    copy_c = send(side.at[x], side.at[2], side_sem.at[1], dest)

    @pl.when(jnp.logical_not(to_self))
    def _():
        copy_c.start()

    @pl.when(jnp.logical_not(to_self))
    def _():
        copy_c.wait_recv()

    @pl.when(to_self)
    def _():
        side[2] = side[x]

    copy_side.wait_recv()
    sides_out[...] = side[...]

    store_wide.wait()
    store_t.wait()
    send(tv.at[theirs, :], tout_hbm.at[:, other_half], tout_sem, partner).wait_recv()
    for copy in sent:
        copy.wait_send()
    edge_up.wait_send()
    edge_down.wait_send()

    @pl.when(jnp.logical_not(to_self))
    def _():
        copy_c.wait_send()


def pair_kernel(
    trunk_hbm, side, wide_hbm, pair_hbm, pb_hbm, tout_hbm, pout_hbm,
    wide, pin, pov, pb, mix, rows_t, trunk, sem, in_sem, out_sem,
):
    loads = [
        pltpu.make_async_copy(src, dst, sem.at[k])
        for k, (src, dst) in enumerate(((wide_hbm, wide), (pb_hbm, pb)))
    ]
    for copy in loads:
        copy.start()
    for b in range(4):
        span = pl.ds(16 * b, 16)
        pltpu.make_async_copy(pair_hbm.at[span], pin.at[span], in_sem.at[b]).start()
    load_t = pltpu.make_async_copy(trunk_hbm, trunk, sem.at[3])
    load_t.start()
    v_of = lax.broadcasted_iota(jnp.int32, (32, 256), 0)
    column = lax.broadcasted_iota(jnp.int32, (32, 256), 1)
    spread = jnp.where(column // 8 == v_of, 1.0, 0.0).astype(BF16)
    s0 = side[0].astype(F32)
    s1 = side[1].astype(F32)
    cs = side[2].astype(F32)
    low = lax.broadcasted_iota(jnp.int32, (16, 128), 1) < 32
    row_t = jnp.concatenate(
        [
            jnp.where(low, s0, pltpu.roll(s1, 32, 1)),
            jnp.where(low, pltpu.roll(s0, 96, 1), s1),
        ],
        axis=0,
    )
    row_side = jnp.transpose(row_t)[0:64].astype(BF16)
    col_t = jnp.concatenate([pltpu.roll(cs, 64, 1), pltpu.roll(cs, 32, 1)], axis=0)
    col_side = jnp.transpose(col_t)[0:32].astype(BF16)
    repeated = jnp.dot(col_side, spread, preferred_element_type=F32)
    for i in range(8):
        mix[32 * i : 32 * i + 32, :] = jnp.where(column % 8 == i, repeated, 0.0).astype(BF16)
    load_t.wait()
    copy_t = pltpu.make_async_copy(trunk, tout_hbm, sem.at[4])
    copy_t.start()
    loads[0].wait()
    rows_t[...] = jnp.dot(row_side, wide[...], preferred_element_type=F32)
    loads[1].wait()
    for g in range(8):
        if g % 2 == 0:
            span = pl.ds(8 * g, 16)
            pltpu.make_async_copy(pair_hbm.at[span], pin.at[span], in_sem.at[g // 2]).wait()
        stack = jnp.concatenate(
            [rows_t[8 * g : 8 * g + 8, 128 * v : 128 * v + 128] for v in range(32)], axis=0
        ).astype(BF16)
        update = jnp.dot(mix[...], stack, preferred_element_type=F32).reshape(8, 32, 128)
        span = slice(8 * g, 8 * g + 8)
        pov[span] = (pin[span].astype(F32) + update + pb[...].reshape(1, 1, 128)).astype(BF16)
        span = pl.ds(8 * g, 8)
        pltpu.make_async_copy(pov.at[span], pout_hbm.at[span], out_sem.at[g]).start()
    for g in range(8):
        span = pl.ds(8 * g, 8)
        pltpu.make_async_copy(pov.at[span], pout_hbm.at[span], out_sem.at[g]).wait()
    copy_t.wait()


VMEM_LIMIT = 60 * 1024 * 1024


def per_device(trunk_in, conv_weight, conv_bias, norm_gain, pair_proj, pair_in, opm_weight, pair_bias):
    hbm = pl.BlockSpec(memory_space=pltpu.HBM)
    dma = pltpu.SemaphoreType.DMA
    trunk, sides, wide = pl.pallas_call(
        kernel,
        name="trunk",
        out_shape=(
            jax.ShapeDtypeStruct(trunk_in.shape, BF16),
            jax.ShapeDtypeStruct((3, 16, 128), BF16),
            jax.ShapeDtypeStruct((32, 4096), BF16),
        ),
        in_specs=[hbm] * 6,
        out_specs=(hbm, pl.BlockSpec(memory_space=pltpu.VMEM), hbm),
        scratch_shapes=[
            pltpu.VMEM((OWN, 1024), BF16),
            pltpu.VMEM((TAPS, 2 * OWN, CH), BF16),
            pltpu.VMEM((NY, OWN, SEG), BF16),
            pltpu.VMEM((NY, OWN, SEG), BF16),
            pltpu.VMEM((OWN, 128), BF16),
            pltpu.VMEM((2, OWN, 128), BF16),
            pltpu.VMEM((NY, 48, 128), BF16),
            pltpu.VMEM((NY, 16, 128), BF16),
            pltpu.VMEM((2, 8, 128), F32),
            pltpu.VMEM((CH, EXT), BF16),
            pltpu.VMEM((CH, 128), F32),
            pltpu.VMEM((8, 128), F32),
            pltpu.VMEM((TAPS, 2 * OWN, EXT), F32),
            pltpu.VMEM((2 * OWN, SEG), F32),
            pltpu.VMEM((2 * OWN, 128), F32),
            pltpu.VMEM((2 * OWN, SEG), BF16),
            pltpu.VMEM((SEG, 128), BF16),
            pltpu.VMEM((64, 2 * OWN), BF16),
            pltpu.VMEM((NY, 32, 128), BF16),
            pltpu.VMEM((3, 16, 128), BF16),
            pltpu.VMEM((1, OWN), F32),
            pltpu.VMEM((12, 128), F32),
            pltpu.VMEM((64, CH), BF16),
            pltpu.VMEM((1024, 128), BF16),
            pltpu.VMEM((1024, 128), F32),
            pltpu.VMEM((32, 4096), BF16),
            dma((10,)),
            dma((2, 2)),
            dma((2,)),
            dma((2,)),
            dma((4, 2)),
            dma((2, 2, 4, 2, 2)),
            dma((2, 4, 2)),
            dma((NY, 2)),
            dma((2, 2)),
            dma((2,)),
            dma((2,)),
            dma((NY, 2)),
            dma((2, 2)),
        ],
        compiler_params=pltpu.CompilerParams(
            collective_id=0, has_side_effects=True, vmem_limit_bytes=VMEM_LIMIT
        ),
        cost_estimate=pl.CostEstimate(
            flops=1_600_000_000, bytes_accessed=3_000_000, transcendentals=1_000_000
        ),
    )(
        trunk_in, conv_weight, conv_bias.reshape(1, OWN), norm_gain.reshape(12, 128), pair_proj,
        opm_weight,
    )
    return pl.pallas_call(
        pair_kernel,
        name="pair",
        out_shape=(
            jax.ShapeDtypeStruct(trunk_in.shape, BF16),
            jax.ShapeDtypeStruct(pair_in.shape, BF16),
        ),
        in_specs=[hbm, pl.BlockSpec(memory_space=pltpu.VMEM), hbm, hbm, hbm],
        out_specs=(hbm, hbm),
        scratch_shapes=[
            pltpu.VMEM((32, 4096), BF16),
            pltpu.VMEM((64, 32, 128), BF16),
            pltpu.VMEM((64, 32, 128), BF16),
            pltpu.VMEM((1, 128), F32),
            pltpu.VMEM((256, 256), BF16),
            pltpu.VMEM((64, 4096), F32),
            pltpu.VMEM((OWN, 1024), BF16),
            dma((5,)),
            dma((4,)),
            dma((8,)),
        ],
        compiler_params=pltpu.CompilerParams(vmem_limit_bytes=VMEM_LIMIT),
        cost_estimate=pl.CostEstimate(flops=200_000_000, bytes_accessed=2_000_000, transcendentals=0),
    )(trunk, sides, wide, pair_in, pair_bias.reshape(1, 128))


def solution(mesh):
    return jax.shard_map(
        per_device,
        mesh=mesh,
        in_specs=(
            P("col", "row"), P(None, "col", None), P("col"), P(), P(), P("row", "col", None), P(), P(),
        ),
        out_specs=(P("col", "row"), P("row", "col", None)),
        check_vma=False,
    )
```

```python
import functools
import jax
import jax.numpy as jnp
from jax import lax
from jax.experimental import pallas as pl
from jax.experimental.pallas import tpu as pltpu
from jax.sharding import PartitionSpec as P

MESH = pl.DeviceIdType.MESH
F32 = jnp.float32
BF16 = jnp.bfloat16

CH = 1536
OWN = 96
SEG = 512
EXT = 640
NY = 8
NROW = 32
TAPS = 5
STEP = 8
EPSILON = 1e-05


def gelu(v):
    u = v * (0.7978845608028654 + 0.035677408136300125 * (v * v))
    h = 0.5 * v
    return h + h * jnp.tanh(u)


def kernel(
    x_hbm, w_hbm, cb_hbm, g_hbm, pp_hbm, opm_hbm,
    tout_hbm, sides_hbm, wide_hbm,
    xv, wbuf, raw_a, raw_b, inner, edge, hal, stat, cbuf, act, gain, sc, taps, acc, bcol,
    tv, pool, own_pp, prow, pcol, mcol, side, cb_ref, g_ref, pp_ref, opm_ref, opm_f, wide,
    local_sem,
    swap_sem, inner_sem, cb_sem, edge_sem, ring_sem, hal_sem, stat_sem, w_sem, sib_sem, tout_sem, row_sem, col_out, col_in,
):
    r = lax.axis_index("row")
    c = lax.axis_index("col")
    x = c // NY
    y = c % NY
    core = r % 2
    up = (r + 1) % NROW
    down = (r + NROW - 1) % NROW
    partner = (r, (1 - x) * NY + y)
    across = (r + 2 - 4 * ((r // 2) % 2), (1 - x) * NY + y)
    sibling = (r + 1 - 2 * core, c)
    ypeer = [(r, x * NY + (y + j) % NY) for j in range(NY)]
    opeer = [(r, (1 - x) * NY + (y + j) % NY) for j in range(NY)]
    window = (r // 8) * 8
    col_dest = 2 * (r % 8) + x
    col_source = [(window + c // 2, (c % 2) * NY + k) for k in range(NY)]
    to_self = col_dest == c
    my_edge = r + 2 * x * 1 - 1
    my_edge = (my_edge + NROW) % NROW

    def send(src, dst, sems, dev):
        return pltpu.make_async_remote_copy(
            src_ref=src, dst_ref=dst, send_sem=sems.at[0], recv_sem=sems.at[1],
            device_id=dev, device_id_type=MESH,
        )

    half = pl.ds(pl.multiple_of(SEG * x, 128), SEG)
    load_x = pltpu.make_async_copy(x_hbm, xv, local_sem.at[0])
    load_a = pltpu.make_async_copy(x_hbm.at[:, half], raw_a.at[y], local_sem.at[1])
    load_w = pltpu.make_async_copy(
        w_hbm, wbuf.at[:, pl.ds(pl.multiple_of(OWN * x, 32), OWN), :], local_sem.at[2]
    )
    tables = [
        pltpu.make_async_copy(src, dst, local_sem.at[5 + k])
        for k, (src, dst) in enumerate(
            ((cb_hbm, cb_ref), (g_hbm, g_ref), (pp_hbm, pp_ref), (opm_hbm, opm_ref))
        )
    ]
    load_x.start()
    load_a.start()
    for copy in tables[:2]:
        copy.start()

    barrier = pltpu.get_barrier_semaphore()
    greet = [partner, across, sibling] + ypeer[1:] + opeer[1:] + [(my_edge, y), (my_edge, NY + y)]
    for dev in greet:
        pl.semaphore_signal(barrier, inc=1, device_id=dev, device_id_type=MESH)

    for k in range(NY):

        @pl.when(jnp.logical_not(jnp.logical_and(to_self, y == k)))
        def _():
            pl.semaphore_signal(barrier, inc=1, device_id=col_source[k], device_id_type=MESH)

    cbuf[pl.ds(x, 1)] = jnp.zeros((1, 8, 128), F32)
    tables[0].wait()
    cbuf[pl.ds(x, 1), :, 0:OWN] = jnp.broadcast_to(cb_ref[...].reshape(1, 1, OWN), (1, 8, OWN))
    load_x.wait()
    load_a.wait()
    pl.semaphore_wait(barrier, len(greet) + NY - jnp.where(to_self, 1, 0))

    sent = []

    def go(copy):
        copy.start()
        sent.append(copy)
        return copy

    def piece_of(kind, owner, piece):
        return (raw_a, raw_b)[kind].at[owner, 48 * piece : 48 * piece + 48]

    def ring(direction, kind, dist, piece):
        owner = (y + NY - (dist - 1)) % NY if direction == 0 else (y + dist - 1) % NY
        at = piece_of(kind, owner, piece)
        dev = ypeer[1] if direction == 0 else ypeer[NY - 1]
        return send(at, at, ring_sem.at[direction, kind, dist - 1, piece], dev)

    def arrived(direction, kind, dist, piece):
        owner = (y + NY - dist) % NY if direction == 0 else (y + dist) % NY
        at = piece_of(kind, owner, piece)
        send(at, at, ring_sem.at[direction, kind, dist - 1, piece], ypeer[1]).wait_recv()

    def step(kind, dist, piece):
        if dist < 4 or kind == 0:
            arrived(0, kind, dist, piece)
            if dist < 3 or (dist == 3 and kind == 0):
                go(ring(0, kind, dist + 1, piece))
        if dist < 4 or kind == 1:
            arrived(1, kind, dist, piece)
            if dist < 3 or (dist == 3 and kind == 1):
                go(ring(1, kind, dist + 1, piece))

    def halo_ring(direction, dist):
        owner = (y + NY - (dist - 1)) % NY if direction == 0 else (y + dist - 1) % NY
        dev = ypeer[1] if direction == 0 else ypeer[NY - 1]
        return send(hal.at[owner], hal.at[owner], hal_sem.at[direction, dist - 1], dev)

    def halo_step(dist):
        for direction in range(2 if dist < 4 else 1):
            owner = (y + NY - dist) % NY if direction == 0 else (y + dist) % NY
            at = hal.at[owner]
            send(at, at, hal_sem.at[direction, dist - 1], ypeer[1]).wait_recv()
            if dist < 3 or (dist == 3 and direction == 0):
                go(halo_ring(direction, dist + 1))

    other = 1 - x
    edge_up = send(xv.at[:, 896:1024], edge.at[x], edge_sem.at[x], (up, y))
    edge_down = send(xv.at[:, 0:128], edge.at[x], edge_sem.at[2 + x], (down, NY + y))
    edge_up.start()
    edge_down.start()
    for piece in range(2):
        for direction in range(2):
            go(ring(direction, 0, 1, piece))
    other_half = pl.ds(pl.multiple_of(SEG * other, 128), SEG)
    copy_swap = [
        go(send(
            xv.at[48 * p : 48 * p + 48, other_half], piece_of(1, y, p), swap_sem.at[p], partner
        ))
        for p in range(2)
    ]
    copy_inner = go(send(
        xv.at[:, pl.ds(pl.multiple_of(SEG - 128 * other, 128), 128)], inner, inner_sem, partner
    ))
    copy_cb = go(send(cbuf.at[x], cbuf.at[x], cb_sem, partner))
    quarters = [pl.ds(pl.multiple_of(768 * core + 384 * q, 128), 384) for q in range(2)]
    mine = pl.ds(pl.multiple_of(OWN * x, 32), OWN)
    theirs = pl.ds(pl.multiple_of(OWN * other, 32), OWN)
    for q, dev in enumerate((partner, across)):
        go(send(w_hbm.at[:, :, quarters[q]], wbuf.at[:, mine, quarters[q]], w_sem.at[q], dev))
    load_w.start()
    for copy in tables[2:]:
        copy.start()

    for piece in range(2):
        step(0, 1, piece)
    for piece in range(2):
        copy_swap[piece].wait_recv()
        go(ring(0, 1, 1, piece))
        go(ring(1, 1, 1, piece))

    copy_inner.wait_recv()
    for k in range(2):

        @pl.when(x == 0)
        def _():
            send(xv.at[:, 896:1024], edge.at[k], edge_sem.at[k], (up, y)).wait_recv()

        @pl.when(x == 1)
        def _():
            send(xv.at[:, 0:128], edge.at[k], edge_sem.at[2 + k], (up, y)).wait_recv()

    own_f = xv[:, half].astype(F32)
    their_f = raw_b[y].astype(F32)
    sums = jnp.sum(own_f * own_f + their_f * their_f, axis=0, keepdims=True)
    at_end = jnp.logical_or(
        jnp.logical_and(x == 0, r == 0), jnp.logical_and(x == 1, r == NROW - 1)
    )
    lane = lax.broadcasted_iota(jnp.int32, (OWN, 128), 1)
    pick_inner = (lane < 64) == (x == 0)
    inner_a = xv[:, pl.ds(pl.multiple_of(SEG - 128 * x, 128), 128)].astype(F32)
    inner_b = inner[...].astype(F32)
    keep = jnp.where(at_end, 0.0, 1.0)
    outer_a = edge[x].astype(F32) * keep
    outer_b = edge[other].astype(F32) * keep
    halo_a = jnp.where(pick_inner, inner_a, outer_a)
    halo_b = jnp.where(pick_inner, inner_b, outer_b)
    halo_sums = jnp.sum(halo_a * halo_a + halo_b * halo_b, axis=0, keepdims=True)
    sums = jnp.concatenate(
        [sums[:, 128 * t : 128 * t + 128] for t in range(4)]
        + [halo_sums, jnp.zeros((3, 128), F32)],
        axis=0,
    )
    rest = sums - sums.astype(BF16).astype(F32)
    stat[y] = jnp.concatenate([sums, rest], axis=0).astype(BF16)
    for j in (4, 3, 5, 2, 6, 1, 7):
        go(send(stat.at[y], stat.at[y], stat_sem.at[j], ypeer[j]))
    lane48 = lax.broadcasted_iota(jnp.int32, (48, 128), 1)
    packed = halo_a[0:48]
    for q, piece in ((1, halo_a[48:96]), (2, halo_b[0:48]), (3, halo_b[48:96])):
        moved = pltpu.roll(piece, 32 * q, 1)
        inside = jnp.logical_and(lane48 >= 32 * q - 16, lane48 < 32 * q + 16)
        packed = jnp.where(inside, moved, packed)
    hal[y] = packed.astype(BF16)
    go(halo_ring(0, 1))
    go(halo_ring(1, 1))

    tables[1].wait()
    for i in range(12):
        gain[128 * i : 128 * i + 128, :] = jnp.transpose(
            jnp.broadcast_to(g_ref[i : i + 1, :], (128, 128))
        )
    for piece in range(2):
        step(0, 2, piece)
    tables[3].wait()
    opm_f[...] = opm_ref[...].astype(F32)
    for v in range(32):
        wide[:, 128 * v : 128 * v + 128] = opm_f[pl.ds(v, 32, stride=32), :].astype(BF16)
    store_wide = pltpu.make_async_copy(wide, wide_hbm, local_sem.at[3])
    store_wide.start()
    for piece in range(2):
        step(1, 1, piece)
    token = lax.broadcasted_iota(jnp.int32, (SEG, 128), 0) // 16
    cell = lax.broadcasted_iota(jnp.int32, (SEG, 128), 1) % 32
    pool[...] = jnp.where(token == cell, 0.0625, 0.0).astype(BF16)
    tables[2].wait()
    channel = lax.broadcasted_iota(jnp.int32, (CH, 2 * OWN), 0)
    place = lax.broadcasted_iota(jnp.int32, (CH, 2 * OWN), 1)
    wanted = place + OWN * y + jnp.where(place >= OWN, 768 - OWN, 0)
    choose = jnp.where(channel == wanted, 1.0, 0.0).astype(BF16)
    own_pp[...] = jnp.dot(pp_ref[...], choose, preferred_element_type=F32).astype(BF16)
    copy_cb.wait_recv()
    for k in range(2):
        bcol[OWN * k : OWN * k + OWN, :] = jnp.transpose(
            jnp.broadcast_to(cbuf[k, 0:1, :], (128, 128))
        )[0:OWN]

    halo_step(1)

    def sums_of(owner):
        both = stat[owner].astype(F32)
        return both[0:8] + both[8:16]

    total = sums_of(y)
    for j in range(1, NY):
        frm = (y + NY - j) % NY
        send(stat.at[y], stat.at[frm], stat_sem.at[j], ypeer[j]).wait_recv()
        total = total + sums_of(frm)
    sc[...] = lax.rsqrt(total * (1.0 / CH) + EPSILON)

    def first_row(kind, owner):
        return ((x if kind == 0 else other) * NY + owner) * OWN

    def activate(kind, owner):
        buf = (raw_a, raw_b)[kind]
        base = first_row(kind, owner)

        for b in range(0, OWN, 16):
            target = pl.ds(pl.multiple_of(base + b, 16), 16)
            g = gain[target, :]
            for t in range(4):
                cols = slice(128 * t, 128 * t + 128)
                v = buf[owner, b : b + 16, cols].astype(F32) * g * sc[t : t + 1, :]
                act[target, cols] = gelu(v).astype(BF16)

    def activate_halo(owner):
        block = hal[owner].astype(F32)
        for q in range(4):
            piece = block if q == 0 else pltpu.roll(block, 128 - 32 * q, 1)
            base = first_row(q // 2, owner) + 48 * (q % 2)
            target = pl.ds(pl.multiple_of(base, 16), 48)
            v = piece * gain[target, :] * sc[4:5, :]
            act[target, SEG:EXT] = gelu(v).astype(BF16)

    def behind(d):
        return (y + NY - d) % NY

    def ahead(d):
        return (y + d) % NY

    for piece in range(2):
        step(0, 3, piece)
    activate(0, y)
    activate(1, y)
    for piece in range(2):
        step(1, 2, piece)
    halo_step(2)
    activate_halo(y)
    for owner in (behind(1), ahead(1)):
        activate(0, owner)
        activate(1, owner)
        activate_halo(owner)
    for owner in (behind(2), ahead(2)):
        activate(0, owner)
    for piece in range(2):
        step(1, 3, piece)
    halo_step(3)
    for q in range(2):
        send(
            w_hbm.at[:, :, quarters[q]], wbuf.at[:, theirs, quarters[q]], w_sem.at[q], partner
        ).wait_recv()
    k_half = pl.ds(pl.multiple_of(768 * core, 128), 768)
    k_rest = pl.ds(pl.multiple_of(768 * (1 - core), 128), 768)
    go(send(wbuf.at[:, theirs, k_half], wbuf.at[:, theirs, k_half], sib_sem, sibling))
    for owner in (behind(2), ahead(2)):
        activate(1, owner)
        activate_halo(owner)
    for owner in (behind(3), ahead(3)):
        activate(0, owner)
        activate(1, owner)
        activate_halo(owner)
    load_w.wait()
    send(wbuf.at[:, theirs, k_rest], wbuf.at[:, theirs, k_rest], sib_sem, sibling).wait_recv()

    def product(tap, group):
        out = None
        for k in range(2):
            span = pl.ds(pl.multiple_of(768 * k + 384 * group, 128), 384)
            term = jnp.dot(wbuf[tap, :, span], act[span, :], preferred_element_type=F32)
            out = term if out is None else out + term
        return out

    group = y // 4

    def early(tap, carry):
        taps[tap] = product(tap, group)
        return carry

    lax.fori_loop(0, TAPS, early, 0)

    for piece in range(2):
        step(0, 4, piece)
    activate(0, behind(4))
    halo_step(4)
    activate_halo(behind(4))
    for piece in range(2):
        step(1, 4, piece)
    activate(1, ahead(4))

    for tap in range(TAPS):
        full = taps[tap] + product(tap, 1 - group)
        delta = STEP * (tap - 2)
        if delta != 0:
            full = pltpu.roll(full, (-delta) % EXT, 1)
        full = full[:, 0:SEG]
        if tap == 0:
            acc[...] = full
        else:
            acc[...] += full

    for t in range(4):
        cols = slice(128 * t, 128 * t + 128)
        own_cols = pl.ds(pl.multiple_of(SEG * x + 128 * t, 128), 128)
        tv[mine, cols] = (
            xv[:, own_cols].astype(F32) + acc[mine, cols] + bcol[mine, :]
        ).astype(BF16)
        tv[theirs, cols] = (
            raw_b[y, :, cols].astype(F32) + acc[theirs, cols] + bcol[theirs, :]
        ).astype(BF16)
    pooled = jnp.dot(tv[...], pool[...], preferred_element_type=F32).astype(BF16)
    pooled_f = pooled.astype(F32)
    squares = jnp.sum(pooled_f * pooled_f, axis=0, keepdims=True)
    proj = jnp.dot(own_pp[...], pooled, preferred_element_type=F32)
    lane_group = lax.broadcasted_iota(jnp.int32, (8, 128), 1) // 32
    squares = jnp.broadcast_to(squares, (8, 128))
    rest = squares - squares.astype(BF16).astype(F32)
    sub = lax.broadcasted_iota(jnp.int32, (8, 128), 0)
    squares = jnp.where(sub < 4, squares, rest)
    folded = []
    for first in (0, 32):
        one = proj[first : first + 8]
        for q in range(1, 4):
            one = jnp.where(lane_group == q, proj[first + 8 * q : first + 8 * q + 8], one)
        folded.append(jnp.concatenate([one, squares], axis=0).astype(BF16))
    prow[x, y] = folded[0]
    mcol[...] = folded[1]
    own = prow.at[x, y]

    def col_copy(k):
        return pltpu.make_async_remote_copy(
            src_ref=mcol, dst_ref=pcol.at[y], send_sem=col_out.at[k], recv_sem=col_in.at[y],
            device_id=(window + k, col_dest), device_id_type=MESH,
        )

    def col_is_self(k):
        return jnp.logical_and(to_self, r % 8 == k)

    for j in (4, 3, 5, 2, 6, 1, 7):
        go(send(own, own, row_sem.at[0, j], ypeer[j]))
        go(send(own, own, row_sem.at[1, j], opeer[j]))
    go(send(own, own, row_sem.at[1, 0], partner))
    for k in range(NY):

        @pl.when(jnp.logical_not(col_is_self(k)))
        def _():
            col_copy(k).start()

    @pl.when(to_self)
    def _():
        pcol[y] = mcol[...]

    copy_t = go(send(tv.at[theirs, :], tout_hbm.at[:, half], tout_sem, partner))
    store_t = pltpu.make_async_copy(tv.at[mine, :], tout_hbm.at[:, half], local_sem.at[4])
    store_t.start()
    def finish(whole):
        norm = lax.rsqrt((whole[8:9] + whole[12:13]) * (1.0 / CH) + EPSILON)
        one = whole[0:8] * norm
        return jnp.concatenate([one, one], axis=0).astype(BF16)

    for column in range(2):
        at = x if column == 0 else other
        whole = None
        for j in range(NY):
            frm = (y + NY - j) % NY
            if column == 1 or j > 0:
                send(own, prow.at[at, frm], row_sem.at[column, j], partner).wait_recv()
            term = prow[at, frm].astype(F32)
            whole = term if whole is None else whole + term
        side[at] = finish(whole)
    whole = None
    for k in range(NY):

        @pl.when(jnp.logical_not(jnp.logical_and(to_self, y == k)))
        def _():
            pltpu.make_async_remote_copy(
                src_ref=mcol, dst_ref=pcol.at[k], send_sem=col_out.at[k], recv_sem=col_in.at[k],
                device_id=partner, device_id_type=MESH,
            ).wait_recv()

        term = pcol[k].astype(F32)
        whole = term if whole is None else whole + term
    side[2] = finish(whole)
    store_s = pltpu.make_async_copy(side, sides_hbm, local_sem.at[9])
    store_s.start()

    store_wide.wait()
    store_t.wait()
    store_s.wait()
    send(tv.at[theirs, :], tout_hbm.at[:, other_half], tout_sem, partner).wait_recv()
    for copy in sent:
        copy.wait_send()
    edge_up.wait_send()
    edge_down.wait_send()

    for k in range(NY):

        @pl.when(jnp.logical_not(col_is_self(k)))
        def _():
            col_copy(k).wait_send()


def pair_kernel(
    trunk_hbm, sides_hbm, wide_hbm, pair_hbm, pb_hbm, tout_hbm, pout_hbm,
    side, wide, pin, pov, pb, mix, rows_t, trunk, sem, in_sem, out_sem,
):
    loads = [
        pltpu.make_async_copy(src, dst, sem.at[k])
        for k, (src, dst) in enumerate(((sides_hbm, side), (wide_hbm, wide), (pb_hbm, pb)))
    ]
    for copy in loads:
        copy.start()
    for b in range(4):
        span = pl.ds(16 * b, 16)
        pltpu.make_async_copy(pair_hbm.at[span], pin.at[span], in_sem.at[b]).start()
    load_t = pltpu.make_async_copy(trunk_hbm, trunk, sem.at[3])
    load_t.start()
    v_of = lax.broadcasted_iota(jnp.int32, (32, 256), 0)
    column = lax.broadcasted_iota(jnp.int32, (32, 256), 1)
    spread = jnp.where(column // 8 == v_of, 1.0, 0.0).astype(BF16)
    loads[0].wait()
    s0 = side[0].astype(F32)[0:8]
    s1 = side[1].astype(F32)[0:8]
    cs = side[2].astype(F32)[0:8]
    low = lax.broadcasted_iota(jnp.int32, (8, 128), 1) < 32

    def turned(block, by):
        return block if by % 128 == 0 else pltpu.roll(block, by % 128, 1)

    row_t = jnp.concatenate(
        [jnp.where(low, turned(s0, -32 * q), turned(s1, 32 - 32 * q)) for q in range(4)], axis=0
    )
    row_side = jnp.transpose(row_t)[0:64].astype(BF16)
    col_t = jnp.concatenate([turned(cs, -32 * q) for q in range(4)], axis=0)
    col_side = jnp.transpose(col_t)[0:32].astype(BF16)
    repeated = jnp.dot(col_side, spread, preferred_element_type=F32)
    for i in range(8):
        mix[32 * i : 32 * i + 32, :] = jnp.where(column % 8 == i, repeated, 0.0).astype(BF16)
    load_t.wait()
    copy_t = pltpu.make_async_copy(trunk, tout_hbm, sem.at[4])
    copy_t.start()
    loads[1].wait()
    rows_t[...] = jnp.dot(row_side, wide[...], preferred_element_type=F32)
    loads[2].wait()
    for g in range(8):
        if g % 2 == 0:
            span = pl.ds(8 * g, 16)
            pltpu.make_async_copy(pair_hbm.at[span], pin.at[span], in_sem.at[g // 2]).wait()
        stack = jnp.concatenate(
            [rows_t[8 * g : 8 * g + 8, 128 * v : 128 * v + 128] for v in range(32)], axis=0
        ).astype(BF16)
        update = jnp.dot(mix[...], stack, preferred_element_type=F32).reshape(8, 32, 128)
        span = slice(8 * g, 8 * g + 8)
        pov[span] = (pin[span].astype(F32) + update + pb[...].reshape(1, 1, 128)).astype(BF16)
        span = pl.ds(8 * g, 8)
        pltpu.make_async_copy(pov.at[span], pout_hbm.at[span], out_sem.at[g]).start()
    for g in range(8):
        span = pl.ds(8 * g, 8)
        pltpu.make_async_copy(pov.at[span], pout_hbm.at[span], out_sem.at[g]).wait()
    copy_t.wait()


VMEM_LIMIT = 60 * 1024 * 1024


def per_device(trunk_in, conv_weight, conv_bias, norm_gain, pair_proj, pair_in, opm_weight, pair_bias):
    hbm = pl.BlockSpec(memory_space=pltpu.HBM)
    dma = pltpu.SemaphoreType.DMA
    trunk, sides, wide = pl.pallas_call(
        kernel,
        name="trunk",
        out_shape=(
            jax.ShapeDtypeStruct(trunk_in.shape, BF16),
            jax.ShapeDtypeStruct((3, 16, 128), BF16),
            jax.ShapeDtypeStruct((32, 4096), BF16),
        ),
        in_specs=[hbm] * 6,
        out_specs=(hbm, hbm, hbm),
        scratch_shapes=[
            pltpu.VMEM((OWN, 1024), BF16),
            pltpu.VMEM((TAPS, 2 * OWN, CH), BF16),
            pltpu.VMEM((NY, OWN, SEG), BF16),
            pltpu.VMEM((NY, OWN, SEG), BF16),
            pltpu.VMEM((OWN, 128), BF16),
            pltpu.VMEM((2, OWN, 128), BF16),
            pltpu.VMEM((NY, 48, 128), BF16),
            pltpu.VMEM((NY, 16, 128), BF16),
            pltpu.VMEM((2, 8, 128), F32),
            pltpu.VMEM((CH, EXT), BF16),
            pltpu.VMEM((CH, 128), F32),
            pltpu.VMEM((8, 128), F32),
            pltpu.VMEM((TAPS, 2 * OWN, EXT), F32),
            pltpu.VMEM((2 * OWN, SEG), F32),
            pltpu.VMEM((2 * OWN, 128), F32),
            pltpu.VMEM((2 * OWN, SEG), BF16),
            pltpu.VMEM((SEG, 128), BF16),
            pltpu.VMEM((64, 2 * OWN), BF16),
            pltpu.VMEM((2, NY, 16, 128), BF16),
            pltpu.VMEM((NY, 16, 128), BF16),
            pltpu.VMEM((16, 128), BF16),
            pltpu.VMEM((3, 16, 128), BF16),
            pltpu.VMEM((1, OWN), F32),
            pltpu.VMEM((12, 128), F32),
            pltpu.VMEM((64, CH), BF16),
            pltpu.VMEM((1024, 128), BF16),
            pltpu.VMEM((1024, 128), F32),
            pltpu.VMEM((32, 4096), BF16),
            dma((10,)),
            dma((2, 2)),
            dma((2,)),
            dma((2,)),
            dma((4, 2)),
            dma((2, 2, 4, 2, 2)),
            dma((2, 4, 2)),
            dma((NY, 2)),
            dma((2, 2)),
            dma((2,)),
            dma((2,)),
            dma((2, NY, 2)),
            dma((NY,)),
            dma((NY,)),
        ],
        compiler_params=pltpu.CompilerParams(
            collective_id=0, has_side_effects=True, vmem_limit_bytes=VMEM_LIMIT
        ),
        cost_estimate=pl.CostEstimate(
            flops=1_600_000_000, bytes_accessed=3_000_000, transcendentals=1_000_000
        ),
    )(
        trunk_in, conv_weight, conv_bias.reshape(1, OWN), norm_gain.reshape(12, 128), pair_proj,
        opm_weight,
    )
    return pl.pallas_call(
        pair_kernel,
        name="pair",
        out_shape=(
            jax.ShapeDtypeStruct(trunk_in.shape, BF16),
            jax.ShapeDtypeStruct(pair_in.shape, BF16),
        ),
        in_specs=[hbm] * 5,
        out_specs=(hbm, hbm),
        scratch_shapes=[
            pltpu.VMEM((3, 16, 128), BF16),
            pltpu.VMEM((32, 4096), BF16),
            pltpu.VMEM((64, 32, 128), BF16),
            pltpu.VMEM((64, 32, 128), BF16),
            pltpu.VMEM((1, 128), F32),
            pltpu.VMEM((256, 256), BF16),
            pltpu.VMEM((64, 4096), F32),
            pltpu.VMEM((OWN, 1024), BF16),
            dma((5,)),
            dma((4,)),
            dma((8,)),
        ],
        compiler_params=pltpu.CompilerParams(vmem_limit_bytes=VMEM_LIMIT),
        cost_estimate=pl.CostEstimate(flops=200_000_000, bytes_accessed=2_000_000, transcendentals=0),
    )(trunk, sides, wide, pair_in, pair_bias.reshape(1, 128))


def solution(mesh):
    return jax.shard_map(
        per_device,
        mesh=mesh,
        in_specs=(
            P("col", "row"), P(None, "col", None), P("col"), P(), P(), P("row", "col", None), P(), P(),
        ),
        out_specs=(P("col", "row"), P("row", "col", None)),
        check_vma=False,
    )
```

```python
import functools
import jax
import jax.numpy as jnp
from jax import lax
from jax.experimental import pallas as pl
from jax.experimental.pallas import tpu as pltpu
from jax.sharding import PartitionSpec as P

MESH = pl.DeviceIdType.MESH
F32 = jnp.float32
BF16 = jnp.bfloat16

CH = 1536
OWN = 96
SEG = 512
EXT = 640
NY = 8
NROW = 32
TAPS = 5
STEP = 8
EPSILON = 1e-05


def gelu(v):
    u = v * (0.7978845608028654 + 0.035677408136300125 * (v * v))
    h = 0.5 * v
    return h + h * jnp.tanh(u)


def kernel(
    x_hbm, w_hbm, cb_hbm, g_hbm, pp_hbm, opm_hbm,
    tout_hbm, sides_hbm, wide_hbm,
    xv, wbuf, raw_a, raw_b, inner, edge, hal, stat, cbuf, act, gain, sc, taps, acc, bcol,
    tv, pool, own_pp, prow, pcol, mcol, side, cb_ref, g_ref, pp_ref, opm_ref, opm_f, wide,
    local_sem,
    swap_sem, inner_sem, cb_sem, edge_sem, ring_sem, hal_sem, stat_sem, w_sem, sib_sem, tout_sem, row_sem, col_out, col_in,
):
    r = lax.axis_index("row")
    c = lax.axis_index("col")
    x = c // NY
    y = c % NY
    core = r % 2
    up = (r + 1) % NROW
    down = (r + NROW - 1) % NROW
    partner = (r, (1 - x) * NY + y)
    across = (r + 2 - 4 * ((r // 2) % 2), (1 - x) * NY + y)
    sibling = (r + 1 - 2 * core, c)
    ypeer = [(r, x * NY + (y + j) % NY) for j in range(NY)]
    opeer = [(r, (1 - x) * NY + (y + j) % NY) for j in range(NY)]
    window = (r // 8) * 8
    col_dest = 2 * (r % 8) + x
    col_source = [(window + c // 2, (c % 2) * NY + k) for k in range(NY)]
    to_self = col_dest == c
    my_edge = r + 2 * x * 1 - 1
    my_edge = (my_edge + NROW) % NROW

    def send(src, dst, sems, dev):
        return pltpu.make_async_remote_copy(
            src_ref=src, dst_ref=dst, send_sem=sems.at[0], recv_sem=sems.at[1],
            device_id=dev, device_id_type=MESH,
        )

    half = pl.ds(pl.multiple_of(SEG * x, 128), SEG)
    load_x = pltpu.make_async_copy(x_hbm, xv, local_sem.at[0])
    load_a = pltpu.make_async_copy(x_hbm.at[:, half], raw_a.at[y], local_sem.at[1])
    load_w = pltpu.make_async_copy(
        w_hbm, wbuf.at[:, pl.ds(pl.multiple_of(OWN * x, 32), OWN), :], local_sem.at[2]
    )
    tables = [
        pltpu.make_async_copy(src, dst, local_sem.at[5 + k])
        for k, (src, dst) in enumerate(
            ((cb_hbm, cb_ref), (g_hbm, g_ref), (pp_hbm, pp_ref), (opm_hbm, opm_ref))
        )
    ]
    load_x.start()
    load_a.start()
    for copy in tables[:2]:
        copy.start()

    barrier = pltpu.get_barrier_semaphore()
    greet = [partner, across, sibling] + ypeer[1:] + opeer[1:] + [(my_edge, y), (my_edge, NY + y)]
    for dev in greet:
        pl.semaphore_signal(barrier, inc=1, device_id=dev, device_id_type=MESH)

    for k in range(NY):

        @pl.when(jnp.logical_not(jnp.logical_and(to_self, y == k)))
        def _():
            pl.semaphore_signal(barrier, inc=1, device_id=col_source[k], device_id_type=MESH)

    cbuf[pl.ds(x, 1)] = jnp.zeros((1, 8, 128), F32)
    tables[0].wait()
    cbuf[pl.ds(x, 1), :, 0:OWN] = jnp.broadcast_to(cb_ref[...].reshape(1, 1, OWN), (1, 8, OWN))
    load_x.wait()
    load_a.wait()
    pl.semaphore_wait(barrier, len(greet) + NY - jnp.where(to_self, 1, 0))

    sent = []

    def go(copy):
        copy.start()
        sent.append(copy)
        return copy

    def piece_of(kind, owner, piece):
        return (raw_a, raw_b)[kind].at[owner, 48 * piece : 48 * piece + 48]

    def ring(direction, kind, dist, piece):
        owner = (y + NY - (dist - 1)) % NY if direction == 0 else (y + dist - 1) % NY
        at = piece_of(kind, owner, piece)
        dev = ypeer[1] if direction == 0 else ypeer[NY - 1]
        return send(at, at, ring_sem.at[direction, kind, dist - 1, piece], dev)

    def arrived(direction, kind, dist, piece):
        owner = (y + NY - dist) % NY if direction == 0 else (y + dist) % NY
        at = piece_of(kind, owner, piece)
        send(at, at, ring_sem.at[direction, kind, dist - 1, piece], ypeer[1]).wait_recv()

    def step(kind, dist, piece):
        if dist < 4 or kind == 0:
            arrived(0, kind, dist, piece)
            if dist < 3 or (dist == 3 and kind == 0):
                go(ring(0, kind, dist + 1, piece))
        if dist < 4 or kind == 1:
            arrived(1, kind, dist, piece)
            if dist < 3 or (dist == 3 and kind == 1):
                go(ring(1, kind, dist + 1, piece))

    def halo_ring(direction, dist):
        owner = (y + NY - (dist - 1)) % NY if direction == 0 else (y + dist - 1) % NY
        dev = ypeer[1] if direction == 0 else ypeer[NY - 1]
        return send(hal.at[owner], hal.at[owner], hal_sem.at[direction, dist - 1], dev)

    def halo_step(dist):
        for direction in range(2 if dist < 4 else 1):
            owner = (y + NY - dist) % NY if direction == 0 else (y + dist) % NY
            at = hal.at[owner]
            send(at, at, hal_sem.at[direction, dist - 1], ypeer[1]).wait_recv()
            if dist < 3 or (dist == 3 and direction == 0):
                go(halo_ring(direction, dist + 1))

    other = 1 - x
    edge_up = send(xv.at[:, 896:1024], edge.at[x], edge_sem.at[x], (up, y))
    edge_down = send(xv.at[:, 0:128], edge.at[x], edge_sem.at[2 + x], (down, NY + y))
    edge_up.start()
    edge_down.start()
    for piece in range(2):
        for direction in range(2):
            go(ring(direction, 0, 1, piece))
    other_half = pl.ds(pl.multiple_of(SEG * other, 128), SEG)
    copy_swap = [
        go(send(
            xv.at[48 * p : 48 * p + 48, other_half], piece_of(1, y, p), swap_sem.at[p], partner
        ))
        for p in range(2)
    ]
    copy_inner = go(send(
        xv.at[:, pl.ds(pl.multiple_of(SEG - 128 * other, 128), 128)], inner, inner_sem, partner
    ))
    copy_cb = go(send(cbuf.at[x], cbuf.at[x], cb_sem, partner))
    quarters = [pl.ds(pl.multiple_of(768 * core + 384 * q, 128), 384) for q in range(2)]
    mine = pl.ds(pl.multiple_of(OWN * x, 32), OWN)
    theirs = pl.ds(pl.multiple_of(OWN * other, 32), OWN)
    for q, dev in enumerate((partner, across)):
        go(send(w_hbm.at[:, :, quarters[q]], wbuf.at[:, mine, quarters[q]], w_sem.at[q], dev))
    load_w.start()
    for copy in tables[2:]:
        copy.start()

    for piece in range(2):
        step(0, 1, piece)
    for piece in range(2):
        copy_swap[piece].wait_recv()
        go(ring(0, 1, 1, piece))
        go(ring(1, 1, 1, piece))

    copy_inner.wait_recv()
    for k in range(2):

        @pl.when(x == 0)
        def _():
            send(xv.at[:, 896:1024], edge.at[k], edge_sem.at[k], (up, y)).wait_recv()

        @pl.when(x == 1)
        def _():
            send(xv.at[:, 0:128], edge.at[k], edge_sem.at[2 + k], (up, y)).wait_recv()

    own_f = xv[:, half].astype(F32)
    their_f = raw_b[y].astype(F32)
    sums = jnp.sum(own_f * own_f + their_f * their_f, axis=0, keepdims=True)
    at_end = jnp.logical_or(
        jnp.logical_and(x == 0, r == 0), jnp.logical_and(x == 1, r == NROW - 1)
    )
    lane = lax.broadcasted_iota(jnp.int32, (OWN, 128), 1)
    pick_inner = (lane < 64) == (x == 0)
    inner_a = xv[:, pl.ds(pl.multiple_of(SEG - 128 * x, 128), 128)].astype(F32)
    inner_b = inner[...].astype(F32)
    keep = jnp.where(at_end, 0.0, 1.0)
    outer_a = edge[x].astype(F32) * keep
    outer_b = edge[other].astype(F32) * keep
    halo_a = jnp.where(pick_inner, inner_a, outer_a)
    halo_b = jnp.where(pick_inner, inner_b, outer_b)
    halo_sums = jnp.sum(halo_a * halo_a + halo_b * halo_b, axis=0, keepdims=True)
    sums = jnp.concatenate(
        [sums[:, 128 * t : 128 * t + 128] for t in range(4)]
        + [halo_sums, jnp.zeros((3, 128), F32)],
        axis=0,
    )
    rest = sums - sums.astype(BF16).astype(F32)
    stat[y] = jnp.concatenate([sums, rest], axis=0).astype(BF16)
    for j in (4, 3, 5, 2, 6, 1, 7):
        go(send(stat.at[y], stat.at[y], stat_sem.at[j], ypeer[j]))
    lane48 = lax.broadcasted_iota(jnp.int32, (48, 128), 1)
    packed = halo_a[0:48]
    for q, piece in ((1, halo_a[48:96]), (2, halo_b[0:48]), (3, halo_b[48:96])):
        moved = pltpu.roll(piece, 32 * q, 1)
        inside = jnp.logical_and(lane48 >= 32 * q - 16, lane48 < 32 * q + 16)
        packed = jnp.where(inside, moved, packed)
    hal[y] = packed.astype(BF16)
    go(halo_ring(0, 1))
    go(halo_ring(1, 1))

    tables[1].wait()
    for i in range(12):
        gain[128 * i : 128 * i + 128, :] = jnp.transpose(
            jnp.broadcast_to(g_ref[i : i + 1, :], (128, 128))
        )
    for piece in range(2):
        step(0, 2, piece)
    tables[3].wait()
    opm_f[...] = opm_ref[...].astype(F32)
    for v in range(32):
        wide[:, 128 * v : 128 * v + 128] = opm_f[pl.ds(v, 32, stride=32), :].astype(BF16)
    store_wide = pltpu.make_async_copy(wide, wide_hbm, local_sem.at[3])
    store_wide.start()
    for piece in range(2):
        step(1, 1, piece)
    token = lax.broadcasted_iota(jnp.int32, (SEG, 128), 0) // 16
    cell = lax.broadcasted_iota(jnp.int32, (SEG, 128), 1) % 32
    pool[...] = jnp.where(token == cell, 0.0625, 0.0).astype(BF16)
    tables[2].wait()
    channel = lax.broadcasted_iota(jnp.int32, (CH, 2 * OWN), 0)
    place = lax.broadcasted_iota(jnp.int32, (CH, 2 * OWN), 1)
    wanted = place + OWN * y + jnp.where(place >= OWN, 768 - OWN, 0)
    choose = jnp.where(channel == wanted, 1.0, 0.0).astype(BF16)
    own_pp[...] = jnp.dot(pp_ref[...], choose, preferred_element_type=F32).astype(BF16)
    copy_cb.wait_recv()
    for k in range(2):
        bcol[OWN * k : OWN * k + OWN, :] = jnp.transpose(
            jnp.broadcast_to(cbuf[k, 0:1, :], (128, 128))
        )[0:OWN]

    halo_step(1)

    def sums_of(owner):
        both = stat[owner].astype(F32)
        return both[0:8] + both[8:16]

    total = sums_of(y)
    for j in range(1, NY):
        frm = (y + NY - j) % NY
        send(stat.at[y], stat.at[frm], stat_sem.at[j], ypeer[j]).wait_recv()
        total = total + sums_of(frm)
    sc[...] = lax.rsqrt(total * (1.0 / CH) + EPSILON)

    def first_row(kind, owner):
        return ((x if kind == 0 else other) * NY + owner) * OWN

    def activate(kind, owner):
        buf = (raw_a, raw_b)[kind]
        base = first_row(kind, owner)

        for b in range(0, OWN, 16):
            target = pl.ds(pl.multiple_of(base + b, 16), 16)
            g = gain[target, :]
            for t in range(4):
                cols = slice(128 * t, 128 * t + 128)
                v = buf[owner, b : b + 16, cols].astype(F32) * g * sc[t : t + 1, :]
                act[target, cols] = gelu(v).astype(BF16)

    def activate_halo(owner):
        block = hal[owner].astype(F32)
        for q in range(4):
            piece = block if q == 0 else pltpu.roll(block, 128 - 32 * q, 1)
            base = first_row(q // 2, owner) + 48 * (q % 2)
            target = pl.ds(pl.multiple_of(base, 16), 48)
            v = piece * gain[target, :] * sc[4:5, :]
            act[target, SEG:EXT] = gelu(v).astype(BF16)

    def behind(d):
        return (y + NY - d) % NY

    def ahead(d):
        return (y + d) % NY

    for piece in range(2):
        step(0, 3, piece)
    activate(0, y)
    activate(1, y)
    for piece in range(2):
        step(1, 2, piece)
    halo_step(2)
    activate_halo(y)
    for owner in (behind(1), ahead(1)):
        activate(0, owner)
        activate(1, owner)
        activate_halo(owner)
    for owner in (behind(2), ahead(2)):
        activate(0, owner)
    for piece in range(2):
        step(1, 3, piece)
    halo_step(3)
    for q in range(2):
        send(
            w_hbm.at[:, :, quarters[q]], wbuf.at[:, theirs, quarters[q]], w_sem.at[q], partner
        ).wait_recv()
    k_half = pl.ds(pl.multiple_of(768 * core, 128), 768)
    k_rest = pl.ds(pl.multiple_of(768 * (1 - core), 128), 768)
    go(send(wbuf.at[:, theirs, k_half], wbuf.at[:, theirs, k_half], sib_sem, sibling))
    for owner in (behind(2), ahead(2)):
        activate(1, owner)
        activate_halo(owner)
    for owner in (behind(3), ahead(3)):
        activate(0, owner)
        activate(1, owner)
        activate_halo(owner)
    load_w.wait()
    send(wbuf.at[:, theirs, k_rest], wbuf.at[:, theirs, k_rest], sib_sem, sibling).wait_recv()

    def product(group):
        out = None
        for k in range(2):
            span = pl.ds(pl.multiple_of(768 * k + 384 * group, 128), 384)
            weights = wbuf[:, :, span].reshape(TAPS * 2 * OWN, 384)
            term = jnp.dot(weights, act[span, :], preferred_element_type=F32)
            out = term if out is None else out + term
        return out.reshape(TAPS, 2 * OWN, EXT)

    group = y // 4
    taps[...] = product(group)

    for piece in range(2):
        step(0, 4, piece)
    activate(0, behind(4))
    halo_step(4)
    activate_halo(behind(4))
    for piece in range(2):
        step(1, 4, piece)
    activate(1, ahead(4))

    late = product(1 - group)
    for tap in range(TAPS):
        full = taps[tap] + late[tap]
        delta = STEP * (tap - 2)
        if delta != 0:
            full = pltpu.roll(full, (-delta) % EXT, 1)
        full = full[:, 0:SEG]
        if tap == 0:
            acc[...] = full
        else:
            acc[...] += full

    for t in range(4):
        cols = slice(128 * t, 128 * t + 128)
        own_cols = pl.ds(pl.multiple_of(SEG * x + 128 * t, 128), 128)
        tv[mine, cols] = (
            xv[:, own_cols].astype(F32) + acc[mine, cols] + bcol[mine, :]
        ).astype(BF16)
        tv[theirs, cols] = (
            raw_b[y, :, cols].astype(F32) + acc[theirs, cols] + bcol[theirs, :]
        ).astype(BF16)
    pooled = jnp.dot(tv[...], pool[...], preferred_element_type=F32).astype(BF16)
    pooled_f = pooled.astype(F32)
    squares = jnp.sum(pooled_f * pooled_f, axis=0, keepdims=True)
    proj = jnp.dot(own_pp[...], pooled, preferred_element_type=F32)
    lane_group = lax.broadcasted_iota(jnp.int32, (8, 128), 1) // 32
    squares = jnp.broadcast_to(squares, (8, 128))
    rest = squares - squares.astype(BF16).astype(F32)
    sub = lax.broadcasted_iota(jnp.int32, (8, 128), 0)
    squares = jnp.where(sub < 4, squares, rest)
    folded = []
    for first in (0, 32):
        one = proj[first : first + 8]
        for q in range(1, 4):
            one = jnp.where(lane_group == q, proj[first + 8 * q : first + 8 * q + 8], one)
        folded.append(jnp.concatenate([one, squares], axis=0).astype(BF16))
    prow[x, y] = folded[0]
    mcol[...] = folded[1]
    own = prow.at[x, y]

    def col_copy(k):
        return pltpu.make_async_remote_copy(
            src_ref=mcol, dst_ref=pcol.at[y], send_sem=col_out.at[k], recv_sem=col_in.at[y],
            device_id=(window + k, col_dest), device_id_type=MESH,
        )

    def col_is_self(k):
        return jnp.logical_and(to_self, r % 8 == k)

    for j in (4, 3, 5, 2, 6, 1, 7):
        go(send(own, own, row_sem.at[0, j], ypeer[j]))
        go(send(own, own, row_sem.at[1, j], opeer[j]))
    go(send(own, own, row_sem.at[1, 0], partner))
    for k in range(NY):

        @pl.when(jnp.logical_not(col_is_self(k)))
        def _():
            col_copy(k).start()

    @pl.when(to_self)
    def _():
        pcol[y] = mcol[...]

    copy_t = go(send(tv.at[theirs, :], tout_hbm.at[:, half], tout_sem, partner))
    store_t = pltpu.make_async_copy(tv.at[mine, :], tout_hbm.at[:, half], local_sem.at[4])
    store_t.start()
    def finish(whole):
        norm = lax.rsqrt((whole[8:9] + whole[12:13]) * (1.0 / CH) + EPSILON)
        one = whole[0:8] * norm
        return jnp.concatenate([one, one], axis=0).astype(BF16)

    for column in range(2):
        at = x if column == 0 else other
        whole = None
        for j in range(NY):
            frm = (y + NY - j) % NY
            if column == 1 or j > 0:
                send(own, prow.at[at, frm], row_sem.at[column, j], partner).wait_recv()
            term = prow[at, frm].astype(F32)
            whole = term if whole is None else whole + term
        side[at] = finish(whole)
    whole = None
    for k in range(NY):

        @pl.when(jnp.logical_not(jnp.logical_and(to_self, y == k)))
        def _():
            pltpu.make_async_remote_copy(
                src_ref=mcol, dst_ref=pcol.at[k], send_sem=col_out.at[k], recv_sem=col_in.at[k],
                device_id=partner, device_id_type=MESH,
            ).wait_recv()

        term = pcol[k].astype(F32)
        whole = term if whole is None else whole + term
    side[2] = finish(whole)
    store_s = pltpu.make_async_copy(side, sides_hbm, local_sem.at[9])
    store_s.start()

    store_wide.wait()
    store_t.wait()
    store_s.wait()
    send(tv.at[theirs, :], tout_hbm.at[:, other_half], tout_sem, partner).wait_recv()
    for copy in sent:
        copy.wait_send()
    edge_up.wait_send()
    edge_down.wait_send()

    for k in range(NY):

        @pl.when(jnp.logical_not(col_is_self(k)))
        def _():
            col_copy(k).wait_send()


def pair_kernel(
    trunk_hbm, sides_hbm, wide_hbm, pair_hbm, pb_hbm, tout_hbm, pout_hbm,
    side, wide, pin, pov, pb, mix, rows_t, trunk, sem, in_sem, out_sem,
):
    loads = [
        pltpu.make_async_copy(src, dst, sem.at[k])
        for k, (src, dst) in enumerate(((sides_hbm, side), (wide_hbm, wide), (pb_hbm, pb)))
    ]
    for copy in loads:
        copy.start()
    for b in range(4):
        span = pl.ds(16 * b, 16)
        pltpu.make_async_copy(pair_hbm.at[span], pin.at[span], in_sem.at[b]).start()
    load_t = pltpu.make_async_copy(trunk_hbm, trunk, sem.at[3])
    load_t.start()
    v_of = lax.broadcasted_iota(jnp.int32, (32, 256), 0)
    column = lax.broadcasted_iota(jnp.int32, (32, 256), 1)
    spread = jnp.where(column // 8 == v_of, 1.0, 0.0).astype(BF16)
    loads[0].wait()
    s0 = side[0].astype(F32)[0:8]
    s1 = side[1].astype(F32)[0:8]
    cs = side[2].astype(F32)[0:8]
    low = lax.broadcasted_iota(jnp.int32, (8, 128), 1) < 32

    def turned(block, by):
        return block if by % 128 == 0 else pltpu.roll(block, by % 128, 1)

    row_t = jnp.concatenate(
        [jnp.where(low, turned(s0, -32 * q), turned(s1, 32 - 32 * q)) for q in range(4)], axis=0
    )
    row_side = jnp.transpose(row_t)[0:64].astype(BF16)
    col_t = jnp.concatenate([turned(cs, -32 * q) for q in range(4)], axis=0)
    col_side = jnp.transpose(col_t)[0:32].astype(BF16)
    repeated = jnp.dot(col_side, spread, preferred_element_type=F32)
    for i in range(8):
        mix[32 * i : 32 * i + 32, :] = jnp.where(column % 8 == i, repeated, 0.0).astype(BF16)
    load_t.wait()
    copy_t = pltpu.make_async_copy(trunk, tout_hbm, sem.at[4])
    copy_t.start()
    loads[1].wait()
    rows_t[...] = jnp.dot(row_side, wide[...], preferred_element_type=F32)
    loads[2].wait()
    for g in range(8):
        if g % 2 == 0:
            span = pl.ds(8 * g, 16)
            pltpu.make_async_copy(pair_hbm.at[span], pin.at[span], in_sem.at[g // 2]).wait()
        stack = jnp.concatenate(
            [rows_t[8 * g : 8 * g + 8, 128 * v : 128 * v + 128] for v in range(32)], axis=0
        ).astype(BF16)
        update = jnp.dot(mix[...], stack, preferred_element_type=F32).reshape(8, 32, 128)
        span = slice(8 * g, 8 * g + 8)
        pov[span] = (pin[span].astype(F32) + update + pb[...].reshape(1, 1, 128)).astype(BF16)
        span = pl.ds(8 * g, 8)
        pltpu.make_async_copy(pov.at[span], pout_hbm.at[span], out_sem.at[g]).start()
    for g in range(8):
        span = pl.ds(8 * g, 8)
        pltpu.make_async_copy(pov.at[span], pout_hbm.at[span], out_sem.at[g]).wait()
    copy_t.wait()


VMEM_LIMIT = 60 * 1024 * 1024


def per_device(trunk_in, conv_weight, conv_bias, norm_gain, pair_proj, pair_in, opm_weight, pair_bias):
    hbm = pl.BlockSpec(memory_space=pltpu.HBM)
    dma = pltpu.SemaphoreType.DMA
    trunk, sides, wide = pl.pallas_call(
        kernel,
        name="trunk",
        out_shape=(
            jax.ShapeDtypeStruct(trunk_in.shape, BF16),
            jax.ShapeDtypeStruct((3, 16, 128), BF16),
            jax.ShapeDtypeStruct((32, 4096), BF16),
        ),
        in_specs=[hbm] * 6,
        out_specs=(hbm, hbm, hbm),
        scratch_shapes=[
            pltpu.VMEM((OWN, 1024), BF16),
            pltpu.VMEM((TAPS, 2 * OWN, CH), BF16),
            pltpu.VMEM((NY, OWN, SEG), BF16),
            pltpu.VMEM((NY, OWN, SEG), BF16),
            pltpu.VMEM((OWN, 128), BF16),
            pltpu.VMEM((2, OWN, 128), BF16),
            pltpu.VMEM((NY, 48, 128), BF16),
            pltpu.VMEM((NY, 16, 128), BF16),
            pltpu.VMEM((2, 8, 128), F32),
            pltpu.VMEM((CH, EXT), BF16),
            pltpu.VMEM((CH, 128), F32),
            pltpu.VMEM((8, 128), F32),
            pltpu.VMEM((TAPS, 2 * OWN, EXT), F32),
            pltpu.VMEM((2 * OWN, SEG), F32),
            pltpu.VMEM((2 * OWN, 128), F32),
            pltpu.VMEM((2 * OWN, SEG), BF16),
            pltpu.VMEM((SEG, 128), BF16),
            pltpu.VMEM((64, 2 * OWN), BF16),
            pltpu.VMEM((2, NY, 16, 128), BF16),
            pltpu.VMEM((NY, 16, 128), BF16),
            pltpu.VMEM((16, 128), BF16),
            pltpu.VMEM((3, 16, 128), BF16),
            pltpu.VMEM((1, OWN), F32),
            pltpu.VMEM((12, 128), F32),
            pltpu.VMEM((64, CH), BF16),
            pltpu.VMEM((1024, 128), BF16),
            pltpu.VMEM((1024, 128), F32),
            pltpu.VMEM((32, 4096), BF16),
            dma((10,)),
            dma((2, 2)),
            dma((2,)),
            dma((2,)),
            dma((4, 2)),
            dma((2, 2, 4, 2, 2)),
            dma((2, 4, 2)),
            dma((NY, 2)),
            dma((2, 2)),
            dma((2,)),
            dma((2,)),
            dma((2, NY, 2)),
            dma((NY,)),
            dma((NY,)),
        ],
        compiler_params=pltpu.CompilerParams(
            collective_id=0, has_side_effects=True, vmem_limit_bytes=VMEM_LIMIT
        ),
        cost_estimate=pl.CostEstimate(
            flops=1_600_000_000, bytes_accessed=3_000_000, transcendentals=1_000_000
        ),
    )(
        trunk_in, conv_weight, conv_bias.reshape(1, OWN), norm_gain.reshape(12, 128), pair_proj,
        opm_weight,
    )
    return pl.pallas_call(
        pair_kernel,
        name="pair",
        out_shape=(
            jax.ShapeDtypeStruct(trunk_in.shape, BF16),
            jax.ShapeDtypeStruct(pair_in.shape, BF16),
        ),
        in_specs=[hbm] * 5,
        out_specs=(hbm, hbm),
        scratch_shapes=[
            pltpu.VMEM((3, 16, 128), BF16),
            pltpu.VMEM((32, 4096), BF16),
            pltpu.VMEM((64, 32, 128), BF16),
            pltpu.VMEM((64, 32, 128), BF16),
            pltpu.VMEM((1, 128), F32),
            pltpu.VMEM((256, 256), BF16),
            pltpu.VMEM((64, 4096), F32),
            pltpu.VMEM((OWN, 1024), BF16),
            dma((5,)),
            dma((4,)),
            dma((8,)),
        ],
        compiler_params=pltpu.CompilerParams(vmem_limit_bytes=VMEM_LIMIT),
        cost_estimate=pl.CostEstimate(flops=200_000_000, bytes_accessed=2_000_000, transcendentals=0),
    )(trunk, sides, wide, pair_in, pair_bias.reshape(1, 128))


def solution(mesh):
    return jax.shard_map(
        per_device,
        mesh=mesh,
        in_specs=(
            P("col", "row"), P(None, "col", None), P("col"), P(), P(), P("row", "col", None), P(), P(),
        ),
        out_specs=(P("col", "row"), P("row", "col", None)),
        check_vma=False,
    )
```
